256 devices in a mesh: blk: 32 (over x, z_hi, core), walker: 8 (over y, z_lo).
Axes of the slice: x: 4, y: 4, z: 8 (z_hi: 4, z_lo: 2; z = z_hi * 2 + z_lo), core: 2. Of those that a mesh axis runs over, the one named last changes fastest.
Arguments:
- measured: bfloat16 [1024, 2, 2, 1440], P(('blk', 'walker')), may hold values from -6 to 6
- slice_q: int32 [64], replicated, may hold values from 0 to 35, as said below
- slice_nu: int32 [64], replicated, may hold values from 0 to 7
- kplusq: int32 [36, 36], replicated, may hold values from 0 to 35, as said below
Outputs:
- four_point: float32 [1152, 64, 2, 1152], P('walker', 'blk')
The draws below stay inside these ranges and needn't reach their ends.
Inputs may be any that keep to these rules, and one draw needn't show every extreme that they name: slice_q takes 8 distinct momenta and slice_nu all 8 bosonic frequencies; every pair of them is one slice, once. kplusq is the addition table of a 6 x 6 periodic momentum grid under a relabelling of the momenta: each row and each column holds every label once, it is symmetric and associative.
All inputs are finite; a program needn't handle non-finite values.
Results may differ from the reference program's by a relative error of at most 0.0003.
Values may be sent and summed in bfloat16 or wider, within the bound.
A program may use at most 128 MiB of HBM per device.

```python
import jax
import jax.numpy as jnp
from jax import lax

SIDE = 6
CLUSTER_MOMENTA = 36
VERTEX_FREQS = 32
NU = 8
NQ = 8
GREEN_FREQS = 40
NSLICE = 64
MEASURE_TOTAL = 1024
MOMENTUM_FREQS = 1152


def slice_table(key):
    order = jax.random.permutation(jax.random.fold_in(key, 101), NSLICE).astype(jnp.int32)
    momenta = jax.random.permutation(jax.random.fold_in(key, 102), CLUSTER_MOMENTA).astype(jnp.int32)[:NQ]
    return (momenta[order // NU].astype(jnp.int32), (order % NU).astype(jnp.int32))


def draw_slice_q(key, part):
    momenta, shifts = slice_table(key)
    return momenta


def draw_slice_nu(key, part):
    momenta, shifts = slice_table(key)
    return shifts


def draw_kplusq(key, part):
    key = jax.random.fold_in(key, 7)
    labels = jax.random.permutation(key, CLUSTER_MOMENTA).astype(jnp.int32)
    element = jnp.argsort(labels).astype(jnp.int32)
    first = element[:, None]
    second = element[None, :]
    row_sum = (first // SIDE + second // SIDE) % SIDE
    col_sum = (first % SIDE + second % SIDE) % SIDE
    return labels[row_sum * SIDE + col_sum].astype(jnp.int32)


def level_of(own_key, dims, split, least, top_value):
    loudness, own = 1.0, jax.random.fold_in(own_key, 6)
    for dim, shards_of in split:
        steps = jnp.exp(jax.random.uniform(jax.random.fold_in(own, dim), (shards_of,), jnp.float32, least / len(split), top_value / len(split)))
        loudness = loudness * jnp.repeat(steps, dims[dim] // shards_of).reshape([-1 if axis == dim else 1 for axis in range(len(dims))])
    return loudness


def centred(stream_key, extent, spread, limit, split=(), held_as=jnp.bfloat16):
    loudness = level_of(stream_key, extent, split, -0.22, 0.18) if split else 1.0
    values = jax.random.normal(stream_key, extent, jnp.float32) * spread * loudness
    return jnp.minimum(jnp.maximum(values, -limit), limit).astype(held_as)


def setup_inputs(seed: int = 0) -> dict:
    splits = jax.random.split(jax.random.key(seed), 5)
    return {
        "measured": centred(splits[0], (MEASURE_TOTAL, 2, 2, CLUSTER_MOMENTA * GREEN_FREQS), 1.0, 6.0, ((0, 256),)),
        "slice_q": draw_slice_q(jax.random.fold_in(splits[4], 71), 0),
        "slice_nu": draw_slice_nu(jax.random.fold_in(splits[4], 71), 0),
        "kplusq": draw_kplusq(jax.random.fold_in(splits[4], 71), 0),
    }


def reference(measured, slice_q, slice_nu, kplusq):
    norm_scale = (2.0 * MEASURE_TOTAL) ** -0.5
    green_block = measured.astype(jnp.float32).reshape(MEASURE_TOTAL, 2, 2, CLUSTER_MOMENTA, GREEN_FREQS)
    unshifted_rows = green_block[:, :, :, :, :VERTEX_FREQS].reshape(MEASURE_TOTAL, 2, 2, MOMENTUM_FREQS)
    left_factor = jnp.concatenate([unshifted_rows[:, :, 0].reshape(2 * MEASURE_TOTAL, MOMENTUM_FREQS), unshifted_rows[:, :, 1].reshape(2 * MEASURE_TOTAL, MOMENTUM_FREQS)], axis=0)

    def one_slice(s):
        q = lax.dynamic_index_in_dim(slice_q, s, 0, keepdims=False)
        momentum_offset = lax.dynamic_index_in_dim(slice_nu, s, 0, keepdims=False)
        shifted_rows = jnp.take(green_block, kplusq[:, q].astype(jnp.int32), axis=3)
        shifted_rows = lax.dynamic_slice_in_dim(shifted_rows, momentum_offset, VERTEX_FREQS, 4).reshape(MEASURE_TOTAL, 2, 2, MOMENTUM_FREQS)
        product_real = shifted_rows[:, :, 0].reshape(2 * MEASURE_TOTAL, MOMENTUM_FREQS)
        product_imaginary = shifted_rows[:, :, 1].reshape(2 * MEASURE_TOTAL, MOMENTUM_FREQS)
        right = jnp.concatenate([jnp.concatenate([product_real, product_imaginary], axis=1), jnp.concatenate([-product_imaginary, product_real], axis=1)], axis=0)
        return jnp.dot(left_factor.T, right, preferred_element_type=jnp.float32, precision=lax.Precision.HIGHEST) * norm_scale

    result = lax.map(one_slice, jnp.arange(NSLICE, dtype=jnp.int32))
    return jnp.transpose(result.reshape(NSLICE, MOMENTUM_FREQS, 2, MOMENTUM_FREQS), (1, 0, 2, 3))
```

```python
import functools

import jax
import jax.numpy as jnp
from jax import lax
from jax.experimental import pallas as pl
from jax.experimental.pallas import tpu as pltpu
from jax.sharding import PartitionSpec as P

MESH = pl.DeviceIdType.MESH
W = 32
G = 40
NX, NZ, NC, NY, NL = 4, 4, 2, 4, 2
NW = NY * NL
ROWS = 144
TILES = 54
XT = 14


def correlate(x_ref, m_ref, nat, rows_f, rows_s, cols_s, rr, gt, hb, other, sib, part, rsr,
              ss_r, rs_r, ss_h, rs_h, ss_g, rs_g, ss_w, rs_w, ss_c, rs_c, ss_x, rs_x,
              ss_z, rs_z, ss_a, rs_a, ss_s, rs_s):
    blk, w = lax.axis_index("blk"), lax.axis_index("walker")
    x, zh, c = blk // (NZ * NC), blk // NC % NZ, blk % NC
    y, zl = w // NL, w % NL

    def dev(x_=x, zh_=zh, c_=c, y_=y, zl_=zl):
        return ((x_ * NZ + zh_) * NC + c_, y_ * NL + zl_)

    def copy(src, dst, send, recv, to):
        return pltpu.make_async_remote_copy(
            src_ref=src, dst_ref=dst, send_sem=send, recv_sem=recv, device_id=to, device_id_type=MESH)

    x_peer = [None] + [lax.rem(x + d, NX) for d in (1, 2, 3)]
    x_from = [None] + [lax.rem(x + NX - d, NX) for d in (1, 2, 3)]
    z_peer = [None] + [lax.rem(zh + d, NZ) for d in (1, 2, 3)]
    z_from = [None] + [lax.rem(zh + NZ - d, NZ) for d in (1, 2, 3)]
    y_peer = [None] + [lax.rem(y + d, NY) for d in (1, 2, 3)]
    y_from = [None] + [lax.rem(y + NY - d, NY) for d in (1, 2, 3)]
    co, lo = 1 - c, 1 - zl
    sibling = dev(c_=co)
    sends = []

    def start(copy_):
        copy_.start()
        sends.append(copy_)

    barrier = pltpu.get_barrier_semaphore()
    peers = [sibling] + [dev(x_=x_peer[d]) for d in (1, 2, 3)] + [dev(zh_=z_peer[d]) for d in (1, 2, 3)]
    w_peer = [None] + [lax.rem(w + d, NW) for d in range(1, NW)]
    w_from = [None] + [lax.rem(w + NW - d, NW) for d in range(1, NW)]
    peers += [(blk, w_peer[d]) for d in range(1, NW)]
    for to in peers:
        pl.semaphore_signal(barrier, inc=1, device_id=to, device_id_type=MESH)

    with jax.named_scope("prep"):
        for i in range(8):
            pair = x_ref[i // 2, i % 2].astype(jnp.float32)
            nat[i:i + 1, :] = pair[0:1]
            nat[i + 8:i + 9, :] = pair[1:2]
        zeros = jnp.zeros((16, 8), jnp.float32)
        for t in range(12):
            tile = jnp.concatenate([nat[:, 120 * t:120 * t + 120], zeros], axis=1)
            cols_s[t // 3, :, 128 * (t % 3):128 * (t % 3) + 128] = tile.astype(jnp.bfloat16)
        for v in range(NW):
            first = 9 * (v // 2) + (5 if v % 2 else 0)
            half = 9 * (v // 2) + 4
            for i in range(4):
                rows_f[:, 32 * i:32 * i + 32] = nat[:, G * (first + i):G * (first + i) + W]
            lane = G * half + 16 * (v % 2)
            rows_f[:, 128:144] = nat[:, lane:lane + 16]
            rows_s[v] = rows_f[...].astype(jnp.bfloat16)

    with jax.named_scope("barrier"):
        pl.semaphore_wait(barrier, len(peers))

    for d in (2, 1, 3):
        start(copy(cols_s.at[z_peer[d]], hb.at[w, zh], ss_h.at[d], rs_h.at[d], dev(zh_=z_peer[d])))
    for d in range(1, NW):
        start(copy(rows_s.at[w_peer[d]], rr.at[w], ss_r.at[d], rs_r.at[d], (blk, w_peer[d])))
    rr[w] = rows_s[w]
    hb[w, zh] = cols_s[zh]

    with jax.named_scope("wait_h"):
        for d in (1, 3, 2):
            slot = hb.at[w, z_from[d]]
            copy(slot, slot, ss_h.at[d], rs_h.at[d], dev(zh_=z_from[d])).wait_recv()
    start(copy(hb.at[w], hb.at[w], ss_w.at[0], rs_w.at[0], dev(zl_=lo)))
    for d in (2, 1, 3):
        start(copy(hb.at[w], hb.at[w], ss_w.at[d], rs_w.at[d], dev(y_=y_peer[d])))

    with jax.named_scope("wait_r"):
        for d in range(1, NW):
            slot = rr.at[w_from[d]]
            copy(slot, slot, ss_r.at[d], rs_r.at[d], (blk, w_from[d])).wait_recv()
    with jax.named_scope("transpose"):
        turned = rr[...].reshape(NW * 16, 256).astype(jnp.float32).T.astype(jnp.bfloat16)
        whole = pl.multiple_of(16 * zl, 16)
        shared = pl.multiple_of(128 * (1 - zl), 16)
        gt[zh, pl.ds(whole, 128), :] = turned[0:128]
        gt[zh, pl.ds(shared, 16), :] = turned[128:144]
    for d in (2, 1, 3):
        start(copy(gt.at[zh], gt.at[zh], ss_g.at[d], rs_g.at[d], dev(zh_=z_peer[d])))

    with jax.named_scope("wait_w0"):
        slot = hb.at[y * NL + lo]
        copy(slot, slot, ss_w.at[0], rs_w.at[0], dev(zl_=lo)).wait_recv()
    for d in (2, 1, 3):
        start(copy(slot, slot, ss_w.at[3 + d], rs_w.at[3 + d], dev(y_=y_peer[d])))

    with jax.named_scope("wait_g"):
        for d in (1, 3, 2):
            slot = gt.at[z_from[d]]
            copy(slot, slot, ss_g.at[d], rs_g.at[d], dev(zh_=z_from[d])).wait_recv()
    left = jnp.concatenate([gt[i] for i in range(NZ)], axis=1).astype(jnp.float32)
    lane = lax.broadcasted_iota(jnp.int32, (ROWS, NZ * 128), 1)
    real = lane % 16 < 8
    left_re = jnp.where(real, left, -left)
    left_im = jnp.where(real, pltpu.roll(left, NZ * 128 - 8, 1), pltpu.roll(left, 8, 1))
    is_re = c == 0
    mine = jnp.where(is_re, left_re, left_im).astype(jnp.bfloat16)
    theirs = jnp.where(is_re, left_im, left_re).astype(jnp.bfloat16)

    with jax.named_scope("wait_w"):
        for d in (1, 3, 2):
            for add, l in ((0, zl), (3, lo)):
                slot = hb.at[y_from[d] * NL + l]
                copy(slot, slot, ss_w.at[add + d], rs_w.at[add + d], dev(y_=y_from[d])).wait_recv()
    with jax.named_scope("dots"):
        right = jnp.concatenate([hb[v, i] for i in range(NZ) for v in range(NW)], axis=0)
        product = jnp.dot(theirs, right, preferred_element_type=jnp.float32)
        for l in range(3):
            other[18 * l:18 * l + 18] = product[:, 128 * l:128 * l + 128].reshape(18, 8, 128)
        other[TILES:] = jnp.zeros((4 * XT - TILES, 8, 128), jnp.float32)
        order = [x_peer[2], x_peer[1], x_peer[3], x]
        for i, at in enumerate(order):
            start(copy(other.at[pl.ds(at * XT, XT)], sib.at[pl.ds(at * XT, XT)], ss_c.at[i], rs_c.at[i], sibling))
        product = jnp.dot(mine, right, preferred_element_type=jnp.float32)
        for l in range(3):
            part[18 * l:18 * l + 18] = product[:, 128 * l:128 * l + 128].reshape(18, 8, 128)
        part[TILES:] = jnp.zeros((4 * XT - TILES, 8, 128), jnp.float32)

    with jax.named_scope("core_sum"):
        for i, (at, d) in enumerate(zip(order, (2, 1, 3, 0))):
            here = pl.ds(at * XT, XT)
            slot = sib.at[here]
            copy(slot, slot, ss_c.at[i], rs_c.at[i], sibling).wait_recv()
            part[here] = part[here] + sib[here]
            if d:
                start(copy(part.at[here], rsr.at[d], ss_x.at[d], rs_x.at[d], dev(x_=at)))
    with jax.named_scope("x_sum"):
        total = part[pl.ds(x * XT, XT)]
        for d in (1, 3, 2):
            copy(rsr.at[d], rsr.at[d], ss_x.at[d], rs_x.at[d], dev(x_=x_from[d])).wait_recv()
            total = total + rsr[d]
        m_ref[c, zh, x] = total * ((2.0 * 1024) ** -0.5)

    def spread(n, zh_):
        slot = m_ref.at[c, zh_, x]
        for d in (2, 1, 3):
            start(copy(slot, slot, ss_a.at[3 * n + d - 1], rs_a.at[3 * n + d - 1], dev(x_=x_peer[d])))
        start(copy(slot, slot, ss_s.at[4 * n], rs_s.at[4 * n], sibling))

    slot = m_ref.at[c, zh, x]
    for d in (2, 1, 3):
        start(copy(slot, slot, ss_z.at[d], rs_z.at[d], dev(zh_=z_peer[d])))
    spread(0, zh)
    with jax.named_scope("z_gather"):
        for d in (1, 3, 2):
            slot = m_ref.at[c, z_from[d], x]
            copy(slot, slot, ss_z.at[d], rs_z.at[d], dev(zh_=z_from[d])).wait_recv()
            spread(d, z_from[d])
    with jax.named_scope("x_gather"):
        for n in (0, 1, 3, 2):
            for d in (1, 3, 2):
                at = zh if n == 0 else z_from[n]
                slot = m_ref.at[c, at, x_from[d]]
                copy(slot, slot, ss_a.at[3 * n + d - 1], rs_a.at[3 * n + d - 1], dev(x_=x_from[d])).wait_recv()
                start(copy(slot, slot, ss_s.at[4 * n + d], rs_s.at[4 * n + d], sibling))
    with jax.named_scope("core_gather"):
        for n in range(4):
            for d in range(4):
                slot = m_ref.at[co, zh if n == 0 else z_from[n], x if d == 0 else x_from[d]]
                copy(slot, slot, ss_s.at[4 * n + d], rs_s.at[4 * n + d], sibling).wait_recv()
    with jax.named_scope("sends"):
        for copy_ in sends:
            copy_.wait_send()


def correlation(measured):
    sem = lambda n: pltpu.SemaphoreType.DMA((n,))
    return pl.pallas_call(
        correlate,
        out_shape=jax.ShapeDtypeStruct((NC, NZ, NX, XT, 8, 128), jnp.float32),
        in_specs=[pl.BlockSpec(memory_space=pltpu.VMEM)],
        out_specs=pl.BlockSpec(memory_space=pltpu.VMEM),
        scratch_shapes=[
            pltpu.VMEM((16, 1440), jnp.float32),
            pltpu.VMEM((16, 256), jnp.float32),
            pltpu.VMEM((NW, 16, 256), jnp.bfloat16),
            pltpu.VMEM((NZ, 16, 384), jnp.bfloat16),
            pltpu.VMEM((NW, 16, 256), jnp.bfloat16),
            pltpu.VMEM((NZ, ROWS, 128), jnp.bfloat16),
            pltpu.VMEM((NW, NZ, 16, 384), jnp.bfloat16),
            pltpu.VMEM((4 * XT, 8, 128), jnp.float32),
            pltpu.VMEM((4 * XT, 8, 128), jnp.float32),
            pltpu.VMEM((4 * XT, 8, 128), jnp.float32),
            pltpu.VMEM((NX, XT, 8, 128), jnp.float32),
            sem(NW), sem(NW), sem(NZ), sem(NZ), sem(NZ), sem(NZ), sem(7), sem(7), sem(4), sem(4),
            sem(NX), sem(NX), sem(NZ), sem(NZ), sem(12), sem(12), sem(16), sem(16),
        ],
        compiler_params=pltpu.CompilerParams(
            collective_id=0, has_side_effects=True, vmem_limit_bytes=16 << 20),
    )(measured)


def select(per_dev, q_ref, nu_ref, kq_ref, m_ref, o_ref):
    base = lax.axis_index("blk") * per_dev
    lane = lax.broadcasted_iota(jnp.int32, (18, 8, 128), 2)

    def column_tile(tile, carry):
        for s in range(per_dev):
            q, nu = q_ref[base + s], nu_ref[base + s]
            parts = [[], []]
            for j in range(4):
                k = kq_ref[tile * 4 + j, q]
                shift = lax.rem(32 * j + 256 - (k % 3) * G - nu, 128)
                for part in range(2):
                    block = m_ref[part, k // 9, pl.ds(k % 9 // 3 * 18, 18)]
                    parts[part].append(pltpu.roll(block, shift, 2))
            for part in range(2):
                a, b, e, f = parts[part]
                row = jnp.where(lane < 64, jnp.where(lane < 32, a, b), jnp.where(lane < 96, e, f))
                o_ref[:, s, part, pl.ds(pl.multiple_of(tile * 128, 128), 128)] = row.reshape(ROWS, 128)
        return carry

    lax.fori_loop(0, 9, column_tile, 0)


def shards(measured, slice_q, slice_nu, kplusq):
    per_dev = slice_q.shape[0] // lax.axis_size("blk")
    m = correlation(measured).reshape(NC, NZ, NX * XT, 8, 128)
    smem, vmem = pl.BlockSpec(memory_space=pltpu.SMEM), pl.BlockSpec(memory_space=pltpu.VMEM)
    return pl.pallas_call(
        functools.partial(select, per_dev),
        out_shape=jax.ShapeDtypeStruct((ROWS, per_dev, 2, 36 * W), jnp.float32),
        in_specs=[smem, smem, smem, vmem],
        out_specs=vmem,
        compiler_params=pltpu.CompilerParams(vmem_limit_bytes=16 << 20),
    )(slice_q, slice_nu, kplusq, m)


def solution(mesh):
    return jax.shard_map(
        shards,
        mesh=mesh,
        in_specs=(P(("blk", "walker"), None, None, None), P(), P(), P()),
        out_specs=P("walker", "blk", None, None),
        check_vma=False,
    )
```

```python
import functools

import jax
import jax.numpy as jnp
from jax import lax
from jax.experimental import pallas as pl
from jax.experimental.pallas import tpu as pltpu
from jax.sharding import PartitionSpec as P

MESH = pl.DeviceIdType.MESH
W = 32
G = 40
NX, NZ, NC, NY, NL = 4, 4, 2, 4, 2
NW = NY * NL
ROWS = 144
TILES = 54
XT = 14
HT = XT // 2 + 1
LN2 = 0.6931471805599453


def encode(values):
    most = jnp.maximum(jnp.max(jnp.abs(values), axis=0), 1e-30)
    power = jnp.floor(jnp.log(most) * (1.0 / LN2)) + 1.0
    scaled = jnp.round(values * jnp.exp((15.0 - power) * LN2)[None])
    scaled = jnp.minimum(jnp.maximum(scaled, -32767.0), 32767.0).reshape(XT // 2, 16, 128)
    powers = jnp.concatenate([power, jnp.zeros_like(power)], axis=0)[None]
    return jnp.concatenate([scaled, powers], axis=0).astype(jnp.int32).astype(jnp.int16)


def decode(coded):
    values = coded.astype(jnp.int32).astype(jnp.float32)
    step = jnp.exp((values[XT // 2, 0:8] - 15.0) * LN2)
    return values[:XT // 2].reshape(XT, 8, 128) * step[None]


def correlate(x_hbm, m_hbm, x_ref, nat, rows_f, rows_s, cols_s, rr, gt, hb, other, sib, part, rsr, mq, ss_l, ss_r, rs_r,
              ss_h, rs_h, ss_g, rs_g, ss_w, rs_w, ss_c, rs_c, ss_x, rs_x, ss_z, rs_z, ss_a, rs_a, ss_s, rs_s, ss_o):
    blk, w = lax.axis_index("blk"), lax.axis_index("walker")
    x, zh, c = blk // (NZ * NC), blk // NC % NZ, blk % NC
    y, zl = w // NL, w % NL
    z = zh * NL + zl

    def dev(x_=x, zh_=zh, c_=c, y_=y, zl_=zl):
        return ((x_ * NZ + zh_) * NC + c_, y_ * NL + zl_)

    def copy(src, dst, send, recv, to):
        return pltpu.make_async_remote_copy(
            src_ref=src, dst_ref=dst, send_sem=send, recv_sem=recv, device_id=to, device_id_type=MESH)

    def ring(at, n):
        return ([at] + [lax.rem(at + d, n) for d in range(1, n)], [at] + [lax.rem(at + n - d, n) for d in range(1, n)])

    x_peer, x_from = ring(x, NX)
    zh_peer, zh_from = ring(zh, NZ)
    y_peer, y_from = ring(y, NY)
    z_peer, z_from = ring(z, NZ * NL)
    w_peer, w_from = ring(w, NW)
    co = 1 - c
    sibling = dev(c_=co)
    sends = []

    def start(copy_):
        copy_.start()
        sends.append(copy_)

    load = pltpu.make_async_copy(x_hbm, x_ref, ss_l.at[0])
    load.start()

    barrier = pltpu.get_barrier_semaphore()
    peers = [dev(zh_=z_peer[d] // NL, zl_=z_peer[d] % NL) for d in (4, 3, 5, 2, 6, 1, 7)]
    peers += [(blk, w_peer[d]) for d in range(1, NW)]
    peers += [dev(x_=x_peer[d]) for d in (1, 2, 3)] + [sibling]
    for to in peers:
        pl.semaphore_signal(barrier, inc=1, device_id=to, device_id_type=MESH)

    load.wait()
    for i in range(8):
        pair = x_ref[i // 2, i % 2].astype(jnp.float32)
        nat[i:i + 1, :] = pair[0:1]
        nat[i + 8:i + 9, :] = pair[1:2]
    for v in range(NW):
        first = 9 * (v // 2) + (5 if v % 2 else 0)
        half = 9 * (v // 2) + 4
        for i in range(4):
            rows_f[:, 32 * i:32 * i + 32] = nat[:, G * (first + i):G * (first + i) + W]
        lane = G * half + 16 * (v % 2)
        rows_f[:, 128:144] = nat[:, lane:lane + 16]
        rows_s[v] = rows_f[...].astype(jnp.bfloat16)
    zeros = jnp.zeros((16, 8), jnp.float32)
    for t in range(12):
        tile = jnp.concatenate([nat[:, 120 * t:120 * t + 120], zeros], axis=1)
        cols_s[t // 3, :, 128 * (t % 3):128 * (t % 3) + 128] = tile.astype(jnp.bfloat16)

    pl.semaphore_wait(barrier, len(peers))

    for d in range(1, NW):
        start(copy(rows_s.at[w_peer[d]], rr.at[w], ss_r.at[d], rs_r.at[d], (blk, w_peer[d])))
    for d in (4, 3, 5, 2, 6, 1, 7):
        to = z_peer[d]
        start(copy(cols_s.at[to // NL], hb.at[y, z], ss_h.at[d], rs_h.at[d], dev(zh_=to // NL, zl_=to % NL)))
    rr[w] = rows_s[w]
    hb[y, z] = cols_s[zh]

    def along_y(n):
        slot = hb.at[y, z_from[n]]
        for d in (2, 1, 3):
            start(copy(slot, slot, ss_w.at[4 * n + d], rs_w.at[4 * n + d], dev(y_=y_peer[d])))

    along_y(0)

    def arrived_h(n):
        slot = hb.at[y, z_from[n]]
        copy(slot, slot, ss_h.at[n], rs_h.at[n], dev(zh_=z_from[n] // NL, zl_=z_from[n] % NL)).wait_recv()
        along_y(n)

    for n in (1, 7, 2, 6):
        arrived_h(n)
    for d in range(1, NW):
        slot = rr.at[w_from[d]]
        copy(slot, slot, ss_r.at[d], rs_r.at[d], (blk, w_from[d])).wait_recv()
    turned = rr[...].reshape(NW * 16, 256).astype(jnp.float32).T.astype(jnp.bfloat16)
    whole = pl.multiple_of(16 * zl, 16)
    shared = pl.multiple_of(128 * (1 - zl), 16)
    gt[zh, pl.ds(whole, 128), :] = turned[0:128]
    gt[zh, pl.ds(shared, 16), :] = turned[128:144]
    for d in (2, 1, 3):
        start(copy(gt.at[zh], gt.at[zh], ss_g.at[d], rs_g.at[d], dev(zh_=zh_peer[d])))
    for n in (3, 5, 4):
        arrived_h(n)

    for n in (0, 1, 7, 2, 6, 3, 5, 4):
        for d in (1, 3, 2):
            slot = hb.at[y_from[d], z_from[n]]
            copy(slot, slot, ss_w.at[4 * n + d], rs_w.at[4 * n + d], dev(y_=y_from[d])).wait_recv()
    for d in (1, 3, 2):
        slot = gt.at[zh_from[d]]
        copy(slot, slot, ss_g.at[d], rs_g.at[d], dev(zh_=zh_from[d])).wait_recv()
    left = jnp.concatenate([gt[i] for i in range(NZ)], axis=1).astype(jnp.float32)
    lane = lax.broadcasted_iota(jnp.int32, (ROWS, NZ * 128), 1)
    real = lane % 16 < 8
    left_re = jnp.where(real, left, -left)
    left_im = jnp.where(real, pltpu.roll(left, NZ * 128 - 8, 1), pltpu.roll(left, 8, 1))
    is_re = c == 0
    mine = jnp.where(is_re, left_re, left_im).astype(jnp.bfloat16)
    theirs = jnp.where(is_re, left_im, left_re).astype(jnp.bfloat16)
    right = jnp.concatenate([hb[v // NL, i * NL + v % NL] for i in range(NZ) for v in range(NW)], axis=0)
    product = jnp.dot(theirs, right, preferred_element_type=jnp.float32)
    for l in range(3):
        other[18 * l:18 * l + 18] = product[:, 128 * l:128 * l + 128].reshape(18, 8, 128)
    other[TILES:] = jnp.zeros((4 * XT - TILES, 8, 128), jnp.float32)
    order = [x_peer[2], x_peer[1], x_peer[3], x]
    for i, at in enumerate(order):
        start(copy(other.at[pl.ds(at * XT, XT)], sib.at[pl.ds(at * XT, XT)], ss_c.at[i], rs_c.at[i], sibling))
    product = jnp.dot(mine, right, preferred_element_type=jnp.float32)
    for l in range(3):
        part[18 * l:18 * l + 18] = product[:, 128 * l:128 * l + 128].reshape(18, 8, 128)
    part[TILES:] = jnp.zeros((4 * XT - TILES, 8, 128), jnp.float32)

    for i, (at, d) in enumerate(zip(order, (2, 1, 3, 0))):
        here = pl.ds(at * XT, XT)
        slot = sib.at[here]
        copy(slot, slot, ss_c.at[i], rs_c.at[i], sibling).wait_recv()
        part[here] = part[here] + sib[here]
        if d:
            start(copy(part.at[here], rsr.at[d], ss_x.at[d], rs_x.at[d], dev(x_=at)))
    total = part[pl.ds(x * XT, XT)]
    for d in (1, 3, 2):
        copy(rsr.at[d], rsr.at[d], ss_x.at[d], rs_x.at[d], dev(x_=x_from[d])).wait_recv()
        total = total + rsr[d]
    mq[zh, x] = encode(total * ((2.0 * 1024) ** -0.5))

    keeps = []

    def arrived(n, d):
        at, slot = (zh_from[n], x_from[d]), mq.at[zh_from[n], x_from[d]]
        start(copy(slot, m_hbm.at[(c, *at)], ss_s.at[4 * n + d], rs_s.at[4 * n + d], sibling))
        keeps.append(pltpu.make_async_copy(slot, m_hbm.at[(c, *at)], ss_o.at[4 * n + d]))
        keeps[-1].start()

    def spread(n):
        slot = mq.at[zh_from[n], x]
        for d in (2, 1, 3):
            start(copy(slot, slot, ss_a.at[4 * n + d], rs_a.at[4 * n + d], dev(x_=x_peer[d])))
        arrived(n, 0)

    slot = mq.at[zh, x]
    for d in (2, 1, 3):
        start(copy(slot, slot, ss_z.at[d], rs_z.at[d], dev(zh_=zh_peer[d])))
    spread(0)
    for n in (1, 3, 2):
        slot = mq.at[zh_from[n], x]
        copy(slot, slot, ss_z.at[n], rs_z.at[n], dev(zh_=zh_from[n])).wait_recv()
        spread(n)
    for n in (0, 1, 3, 2):
        for d in (1, 3, 2):
            slot = mq.at[zh_from[n], x_from[d]]
            copy(slot, slot, ss_a.at[4 * n + d], rs_a.at[4 * n + d], dev(x_=x_from[d])).wait_recv()
            arrived(n, d)
    for copy_ in keeps:
        copy_.wait()
    for n in range(NZ):
        for d in range(NX):
            slot = m_hbm.at[co, zh_from[n], x_from[d]]
            copy(slot, slot, ss_s.at[4 * n + d], rs_s.at[4 * n + d], sibling).wait_recv()
    for copy_ in sends:
        copy_.wait_send()


def correlation(measured):
    sem = lambda n: pltpu.SemaphoreType.DMA((n,))
    return pl.pallas_call(
        correlate,
        out_shape=jax.ShapeDtypeStruct((NC, NZ, NX, HT, 16, 128), jnp.int16),
        in_specs=[pl.BlockSpec(memory_space=pltpu.HBM)],
        out_specs=pl.BlockSpec(memory_space=pltpu.HBM),
        scratch_shapes=[
            pltpu.VMEM(measured.shape, jnp.bfloat16),
            pltpu.VMEM((16, 1440), jnp.float32),
            pltpu.VMEM((16, 256), jnp.float32),
            pltpu.VMEM((NW, 16, 256), jnp.bfloat16),
            pltpu.VMEM((NZ, 16, 384), jnp.bfloat16),
            pltpu.VMEM((NW, 16, 256), jnp.bfloat16),
            pltpu.VMEM((NZ, ROWS, 128), jnp.bfloat16),
            pltpu.VMEM((NY, NZ * NL, 16, 384), jnp.bfloat16),
            pltpu.VMEM((4 * XT, 8, 128), jnp.float32),
            pltpu.VMEM((4 * XT, 8, 128), jnp.float32),
            pltpu.VMEM((4 * XT, 8, 128), jnp.float32),
            pltpu.VMEM((NX, XT, 8, 128), jnp.float32),
            pltpu.VMEM((NZ, NX, HT, 16, 128), jnp.int16),
            sem(1), sem(NW), sem(NW), sem(8), sem(8), sem(NZ), sem(NZ), sem(32), sem(32), sem(4), sem(4),
            sem(NX), sem(NX), sem(NZ), sem(NZ), sem(16), sem(16), sem(16), sem(16), sem(16),
        ],
        compiler_params=pltpu.CompilerParams(
            collective_id=0, has_side_effects=True, vmem_limit_bytes=60 << 20),
    )(measured)


def select(per_dev, q_hbm, nu_hbm, kq_hbm, mq_hbm, o_hbm, q_ref, nu_ref, kq_ref, mq, m_ref, o_ref, ss_l, ss_m, ss_o):
    tables = [pltpu.make_async_copy(src, dst, ss_l.at[i])
              for i, (src, dst) in enumerate(((q_hbm, q_ref), (nu_hbm, nu_ref), (kq_hbm, kq_ref)))]
    blocks = [pltpu.make_async_copy(mq_hbm.at[ri, zh], mq.at[ri, zh], ss_m.at[ri * NZ + zh])
              for ri in range(2) for zh in range(NZ)]
    for copy_ in blocks + tables:
        copy_.start()
    for ri in range(2):
        for zh in range(NZ):
            blocks[ri * NZ + zh].wait()
            for x in range(NX):
                m_ref[ri, zh, x * XT:(x + 1) * XT] = decode(mq[ri, zh, x])
    for copy_ in tables:
        copy_.wait()

    base = lax.axis_index("blk") * per_dev
    lane = lax.broadcasted_iota(jnp.int32, (18, 8, 128), 2)

    def out(tile, s):
        lanes = pl.ds(pl.multiple_of(tile * 128, 128), 128)
        return pltpu.make_async_copy(o_ref.at[tile, s], o_hbm.at[:, s, :, lanes], ss_o.at[tile * per_dev + s])

    def column_tile(tile, carry):
        for s in range(per_dev):
            q, nu = q_ref[base + s], nu_ref[base + s]
            parts = [[], []]
            for j in range(4):
                k = kq_ref[tile * 4 + j, q]
                shift = lax.rem(32 * j + 256 - (k % 3) * G - nu, 128)
                for ri in range(2):
                    block = m_ref[ri, k // 9, pl.ds(k % 9 // 3 * 18, 18)]
                    parts[ri].append(pltpu.roll(block, shift, 2))
            for ri in range(2):
                a, b, e, f = parts[ri]
                row = jnp.where(lane < 64, jnp.where(lane < 32, a, b), jnp.where(lane < 96, e, f))
                o_ref[tile, s, :, ri, :] = row.reshape(ROWS, 128)
            out(tile, s).start()
        return carry

    lax.fori_loop(0, 9, column_tile, 0)
    for tile in range(9):
        for s in range(per_dev):
            out(tile, s).wait()


def shards(measured, slice_q, slice_nu, kplusq):
    per_dev = slice_q.shape[0] // lax.axis_size("blk")
    sem = lambda n: pltpu.SemaphoreType.DMA((n,))
    return pl.pallas_call(
        functools.partial(select, per_dev),
        out_shape=jax.ShapeDtypeStruct((ROWS, per_dev, 2, 36 * W), jnp.float32),
        in_specs=[pl.BlockSpec(memory_space=pltpu.HBM)] * 4,
        out_specs=pl.BlockSpec(memory_space=pltpu.HBM),
        scratch_shapes=[
            pltpu.SMEM(slice_q.shape, jnp.int32),
            pltpu.SMEM(slice_nu.shape, jnp.int32),
            pltpu.SMEM(kplusq.shape, jnp.int32),
            pltpu.VMEM((NC, NZ, NX, HT, 16, 128), jnp.int16),
            pltpu.VMEM((NC, NZ, NX * XT, 8, 128), jnp.float32),
            pltpu.VMEM((9, per_dev, ROWS, 2, 128), jnp.float32),
            sem(3), sem(NC * NZ), sem(9 * per_dev),
        ],
        compiler_params=pltpu.CompilerParams(vmem_limit_bytes=60 << 20),
    )(slice_q, slice_nu, kplusq, correlation(measured))


def solution(mesh):
    return jax.shard_map(
        shards,
        mesh=mesh,
        in_specs=(P(("blk", "walker"), None, None, None), P(), P(), P()),
        out_specs=P("walker", "blk", None, None),
        check_vma=False,
    )
```

```python
import functools

import jax
import jax.numpy as jnp
from jax import lax
from jax.experimental import pallas as pl
from jax.experimental.pallas import tpu as pltpu
from jax.sharding import PartitionSpec as P

MESH = pl.DeviceIdType.MESH
W = 32
G = 40
NX, NZ, NC, NY, NL = 4, 4, 2, 4, 2
NW = NY * NL
ROWS = 144
TILES = 54
XT = 14
HT = XT // 2 + 1
LN2 = 0.6931471805599453


def encode(values):
    most = jnp.maximum(jnp.max(jnp.abs(values), axis=0), 1e-30)
    power = jnp.floor(jnp.log(most) * (1.0 / LN2)) + 1.0
    scaled = jnp.round(values * jnp.exp((15.0 - power) * LN2)[None])
    scaled = jnp.minimum(jnp.maximum(scaled, -32767.0), 32767.0).reshape(XT // 2, 16, 128)
    powers = jnp.concatenate([power, jnp.zeros_like(power)], axis=0)[None]
    return jnp.concatenate([scaled, powers], axis=0).astype(jnp.int32).astype(jnp.int16)


def decode(coded):
    values = coded.astype(jnp.int32).astype(jnp.float32)
    step = jnp.exp((values[XT // 2, 0:8] - 15.0) * LN2)
    return values[:XT // 2].reshape(XT, 8, 128) * step[None]


def correlate(x_hbm, m_hbm, x_ref, nat, rows_f, rows_s, cols_s, rr, gt, hb, other, sib, part, sent, rsr, mq, ss_l, ss_r, rs_r,
              ss_h, rs_h, ss_g, rs_g, ss_w, rs_w, ss_c, rs_c, ss_x, rs_x, ss_z, rs_z, ss_a, rs_a, ss_s, rs_s, ss_o):
    blk, w = lax.axis_index("blk"), lax.axis_index("walker")
    x, zh, c = blk // (NZ * NC), blk // NC % NZ, blk % NC
    y, zl = w // NL, w % NL
    z = zh * NL + zl

    def dev(x_=x, zh_=zh, c_=c, y_=y, zl_=zl):
        return ((x_ * NZ + zh_) * NC + c_, y_ * NL + zl_)

    def copy(src, dst, send, recv, to):
        return pltpu.make_async_remote_copy(
            src_ref=src, dst_ref=dst, send_sem=send, recv_sem=recv, device_id=to, device_id_type=MESH)

    def ring(at, n):
        return ([at] + [lax.rem(at + d, n) for d in range(1, n)], [at] + [lax.rem(at + n - d, n) for d in range(1, n)])

    x_peer, x_from = ring(x, NX)
    zh_peer, zh_from = ring(zh, NZ)
    y_peer, y_from = ring(y, NY)
    z_peer, z_from = ring(z, NZ * NL)
    w_peer, w_from = ring(w, NW)
    co = 1 - c
    sibling = dev(c_=co)
    sends = []

    def start(copy_):
        copy_.start()
        sends.append(copy_)

    load = pltpu.make_async_copy(x_hbm, x_ref, ss_l.at[0])
    load.start()

    barrier = pltpu.get_barrier_semaphore()
    peers = [dev(zh_=z_peer[d] // NL, zl_=z_peer[d] % NL) for d in (4, 3, 5, 2, 6, 1, 7)]
    peers += [(blk, w_peer[d]) for d in range(1, NW)]
    peers += [dev(x_=x_peer[d]) for d in (1, 2, 3)] + [sibling]
    for to in peers:
        pl.semaphore_signal(barrier, inc=1, device_id=to, device_id_type=MESH)

    load.wait()
    for i in range(8):
        pair = x_ref[i // 2, i % 2].astype(jnp.float32)
        nat[i:i + 1, :] = pair[0:1]
        nat[i + 8:i + 9, :] = pair[1:2]
    for v in range(NW):
        first = 9 * (v // 2) + (5 if v % 2 else 0)
        half = 9 * (v // 2) + 4
        for i in range(4):
            rows_f[:, 32 * i:32 * i + 32] = nat[:, G * (first + i):G * (first + i) + W]
        lane = G * half + 16 * (v % 2)
        rows_f[:, 128:144] = nat[:, lane:lane + 16]
        rows_s[v] = rows_f[...].astype(jnp.bfloat16)
    zeros = jnp.zeros((16, 8), jnp.float32)
    for t in range(12):
        tile = jnp.concatenate([nat[:, 120 * t:120 * t + 120], zeros], axis=1)
        cols_s[t // 3, :, 128 * (t % 3):128 * (t % 3) + 128] = tile.astype(jnp.bfloat16)

    pl.semaphore_wait(barrier, len(peers))

    for d in range(1, NW):
        start(copy(rows_s.at[w_peer[d]], rr.at[w], ss_r.at[d], rs_r.at[d], (blk, w_peer[d])))
    for d in (1, 7, 2, 6, 3, 5, 4):
        to = z_peer[d]
        start(copy(cols_s.at[to // NL], hb.at[y, z], ss_h.at[d], rs_h.at[d], dev(zh_=to // NL, zl_=to % NL)))
    rr[w] = rows_s[w]
    hb[y, z] = cols_s[zh]

    def along_y(n):
        slot = hb.at[y, z_from[n]]
        for d in (2, 1, 3):
            start(copy(slot, slot, ss_w.at[4 * n + d], rs_w.at[4 * n + d], dev(y_=y_peer[d])))

    along_y(0)

    def arrived_h(n):
        slot = hb.at[y, z_from[n]]
        copy(slot, slot, ss_h.at[n], rs_h.at[n], dev(zh_=z_from[n] // NL, zl_=z_from[n] % NL)).wait_recv()
        along_y(n)

    for n in (1, 7, 2, 6):
        arrived_h(n)
    for d in range(1, NW):
        slot = rr.at[w_from[d]]
        copy(slot, slot, ss_r.at[d], rs_r.at[d], (blk, w_from[d])).wait_recv()
    turned = rr[...].reshape(NW * 16, 256).astype(jnp.float32).T.astype(jnp.bfloat16)
    whole = pl.multiple_of(16 * zl, 16)
    shared = pl.multiple_of(128 * (1 - zl), 16)
    gt[zh, pl.ds(whole, 128), :] = turned[0:128]
    gt[zh, pl.ds(shared, 16), :] = turned[128:144]
    for d in (2, 1, 3):
        start(copy(gt.at[zh], gt.at[zh], ss_g.at[d], rs_g.at[d], dev(zh_=zh_peer[d])))
    for n in (3, 5, 4):
        arrived_h(n)

    for n in (0, 1, 7, 2, 6, 3, 5, 4):
        for d in (1, 3, 2):
            slot = hb.at[y_from[d], z_from[n]]
            copy(slot, slot, ss_w.at[4 * n + d], rs_w.at[4 * n + d], dev(y_=y_from[d])).wait_recv()
    for d in (1, 3, 2):
        slot = gt.at[zh_from[d]]
        copy(slot, slot, ss_g.at[d], rs_g.at[d], dev(zh_=zh_from[d])).wait_recv()
    left = jnp.concatenate([gt[i] for i in range(NZ)], axis=1).astype(jnp.float32)
    lane = lax.broadcasted_iota(jnp.int32, (ROWS, NZ * 128), 1)
    real = lane % 16 < 8
    left_re = jnp.where(real, left, -left)
    left_im = jnp.where(real, pltpu.roll(left, NZ * 128 - 8, 1), pltpu.roll(left, 8, 1))
    is_re = c == 0
    mine = jnp.where(is_re, left_re, left_im).astype(jnp.bfloat16)
    theirs = jnp.where(is_re, left_im, left_re).astype(jnp.bfloat16)
    right = jnp.concatenate([hb[v // NL, i * NL + v % NL] for i in range(NZ) for v in range(NW)], axis=0)
    product = jnp.dot(theirs, right, preferred_element_type=jnp.float32)
    for l in range(3):
        other[18 * l:18 * l + 18] = product[:, 128 * l:128 * l + 128].reshape(18, 8, 128)
    other[TILES:] = jnp.zeros((4 * XT - TILES, 8, 128), jnp.float32)
    order = [x_peer[2], x_peer[1], x_peer[3], x]
    for i, at in enumerate(order):
        start(copy(other.at[pl.ds(at * XT, XT)], sib.at[pl.ds(at * XT, XT)], ss_c.at[i], rs_c.at[i], sibling))
    product = jnp.dot(mine, right, preferred_element_type=jnp.float32)
    for l in range(3):
        part[18 * l:18 * l + 18] = product[:, 128 * l:128 * l + 128].reshape(18, 8, 128)
    part[TILES:] = jnp.zeros((4 * XT - TILES, 8, 128), jnp.float32)

    for i, (at, d) in enumerate(zip(order, (2, 1, 3, 0))):
        here = pl.ds(at * XT, XT)
        slot = sib.at[here]
        copy(slot, slot, ss_c.at[i], rs_c.at[i], sibling).wait_recv()
        total = part[here] + sib[here]
        if d:
            sent[d] = encode(total)
            start(copy(sent.at[d], rsr.at[d], ss_x.at[d], rs_x.at[d], dev(x_=at)))
    for d in (1, 3, 2):
        copy(rsr.at[d], rsr.at[d], ss_x.at[d], rs_x.at[d], dev(x_=x_from[d])).wait_recv()
        total = total + decode(rsr[d])
    mq[zh, x] = encode(total * ((2.0 * 1024) ** -0.5))

    keeps = []

    def arrived(n, d):
        at, slot = (zh_from[n], x_from[d]), mq.at[zh_from[n], x_from[d]]
        start(copy(slot, m_hbm.at[(c, *at)], ss_s.at[4 * n + d], rs_s.at[4 * n + d], sibling))
        keeps.append(pltpu.make_async_copy(slot, m_hbm.at[(c, *at)], ss_o.at[4 * n + d]))
        keeps[-1].start()

    def spread(n):
        slot = mq.at[zh_from[n], x]
        for d in (2, 1, 3):
            start(copy(slot, slot, ss_a.at[4 * n + d], rs_a.at[4 * n + d], dev(x_=x_peer[d])))
        arrived(n, 0)

    slot = mq.at[zh, x]
    for d in (1, 3, 2):
        start(copy(slot, slot, ss_z.at[d], rs_z.at[d], dev(zh_=zh_peer[d])))
    spread(0)
    for n in (1, 3, 2):
        slot = mq.at[zh_from[n], x]
        copy(slot, slot, ss_z.at[n], rs_z.at[n], dev(zh_=zh_from[n])).wait_recv()
        spread(n)
    for n in (0, 1, 3, 2):
        for d in (1, 3, 2):
            slot = mq.at[zh_from[n], x_from[d]]
            copy(slot, slot, ss_a.at[4 * n + d], rs_a.at[4 * n + d], dev(x_=x_from[d])).wait_recv()
            arrived(n, d)
    for copy_ in keeps:
        copy_.wait()
    for n in range(NZ):
        for d in range(NX):
            slot = m_hbm.at[co, zh_from[n], x_from[d]]
            copy(slot, slot, ss_s.at[4 * n + d], rs_s.at[4 * n + d], sibling).wait_recv()
    for copy_ in sends:
        copy_.wait_send()


def correlation(measured):
    sem = lambda n: pltpu.SemaphoreType.DMA((n,))
    return pl.pallas_call(
        correlate,
        out_shape=jax.ShapeDtypeStruct((NC, NZ, NX, HT, 16, 128), jnp.int16),
        in_specs=[pl.BlockSpec(memory_space=pltpu.HBM)],
        out_specs=pl.BlockSpec(memory_space=pltpu.HBM),
        scratch_shapes=[
            pltpu.VMEM(measured.shape, jnp.bfloat16),
            pltpu.VMEM((16, 1440), jnp.float32),
            pltpu.VMEM((16, 256), jnp.float32),
            pltpu.VMEM((NW, 16, 256), jnp.bfloat16),
            pltpu.VMEM((NZ, 16, 384), jnp.bfloat16),
            pltpu.VMEM((NW, 16, 256), jnp.bfloat16),
            pltpu.VMEM((NZ, ROWS, 128), jnp.bfloat16),
            pltpu.VMEM((NY, NZ * NL, 16, 384), jnp.bfloat16),
            pltpu.VMEM((4 * XT, 8, 128), jnp.float32),
            pltpu.VMEM((4 * XT, 8, 128), jnp.float32),
            pltpu.VMEM((4 * XT, 8, 128), jnp.float32),
            pltpu.VMEM((NX, HT, 16, 128), jnp.int16),
            pltpu.VMEM((NX, HT, 16, 128), jnp.int16),
            pltpu.VMEM((NZ, NX, HT, 16, 128), jnp.int16),
            sem(1), sem(NW), sem(NW), sem(8), sem(8), sem(NZ), sem(NZ), sem(32), sem(32), sem(4), sem(4),
            sem(NX), sem(NX), sem(NZ), sem(NZ), sem(16), sem(16), sem(16), sem(16), sem(16),
        ],
        compiler_params=pltpu.CompilerParams(
            collective_id=0, has_side_effects=True, vmem_limit_bytes=60 << 20),
    )(measured)


def select(per_dev, q_hbm, nu_hbm, kq_hbm, mq_hbm, o_hbm, q_ref, nu_ref, kq_ref, mq, m_ref, o_ref, ss_l, ss_m, ss_o):
    tables = [pltpu.make_async_copy(src, dst, ss_l.at[i])
              for i, (src, dst) in enumerate(((q_hbm, q_ref), (nu_hbm, nu_ref), (kq_hbm, kq_ref)))]
    blocks = [pltpu.make_async_copy(mq_hbm.at[ri, zh], mq.at[ri, zh], ss_m.at[ri * NZ + zh])
              for ri in range(2) for zh in range(NZ)]
    for copy_ in blocks + tables:
        copy_.start()
    for ri in range(2):
        for zh in range(NZ):
            blocks[ri * NZ + zh].wait()
            for x in range(NX):
                m_ref[ri, zh, x * XT:(x + 1) * XT] = decode(mq[ri, zh, x])
    for copy_ in tables:
        copy_.wait()

    base = lax.axis_index("blk") * per_dev
    lane = lax.broadcasted_iota(jnp.int32, (18, 8, 128), 2)

    def out(tile, s):
        lanes = pl.ds(pl.multiple_of(tile * 128, 128), 128)
        return pltpu.make_async_copy(o_ref.at[tile, s], o_hbm.at[:, s, :, lanes], ss_o.at[tile * per_dev + s])

    def column_tile(tile, carry):
        for s in range(per_dev):
            q, nu = q_ref[base + s], nu_ref[base + s]
            parts = [[], []]
            for j in range(4):
                k = kq_ref[tile * 4 + j, q]
                shift = lax.rem(32 * j + 256 - (k % 3) * G - nu, 128)
                for ri in range(2):
                    block = m_ref[ri, k // 9, pl.ds(k % 9 // 3 * 18, 18)]
                    parts[ri].append(pltpu.roll(block, shift, 2))
            for ri in range(2):
                a, b, e, f = parts[ri]
                row = jnp.where(lane < 64, jnp.where(lane < 32, a, b), jnp.where(lane < 96, e, f))
                o_ref[tile, s, :, ri, :] = row.reshape(ROWS, 128)
            out(tile, s).start()
        return carry

    lax.fori_loop(0, 9, column_tile, 0, unroll=True)
    for tile in range(9):
        for s in range(per_dev):
            out(tile, s).wait()


def shards(measured, slice_q, slice_nu, kplusq):
    per_dev = slice_q.shape[0] // lax.axis_size("blk")
    sem = lambda n: pltpu.SemaphoreType.DMA((n,))
    return pl.pallas_call(
        functools.partial(select, per_dev),
        out_shape=jax.ShapeDtypeStruct((ROWS, per_dev, 2, 36 * W), jnp.float32),
        in_specs=[pl.BlockSpec(memory_space=pltpu.HBM)] * 4,
        out_specs=pl.BlockSpec(memory_space=pltpu.HBM),
        scratch_shapes=[
            pltpu.SMEM(slice_q.shape, jnp.int32),
            pltpu.SMEM(slice_nu.shape, jnp.int32),
            pltpu.SMEM(kplusq.shape, jnp.int32),
            pltpu.VMEM((NC, NZ, NX, HT, 16, 128), jnp.int16),
            pltpu.VMEM((NC, NZ, NX * XT, 8, 128), jnp.float32),
            pltpu.VMEM((9, per_dev, ROWS, 2, 128), jnp.float32),
            sem(3), sem(NC * NZ), sem(9 * per_dev),
        ],
        compiler_params=pltpu.CompilerParams(vmem_limit_bytes=60 << 20),
    )(slice_q, slice_nu, kplusq, correlation(measured))


def solution(mesh):
    return jax.shard_map(
        shards,
        mesh=mesh,
        in_specs=(P(("blk", "walker"), None, None, None), P(), P(), P()),
        out_specs=P("walker", "blk", None, None),
        check_vma=False,
    )
```

```python
import functools

import jax
import jax.numpy as jnp
from jax import lax
from jax.experimental import pallas as pl
from jax.experimental.pallas import tpu as pltpu
from jax.sharding import PartitionSpec as P

MESH = pl.DeviceIdType.MESH
W = 32
G = 40
NX, NZ, NC, NY, NL = 4, 4, 2, 4, 2
NW = NY * NL
ROWS = 144
TILES = 54
XT = 14
HT = XT // 2 + 1
LN2 = 0.6931471805599453


def encode(values):
    most = jnp.maximum(jnp.max(jnp.abs(values), axis=0), 1e-30)
    power = jnp.floor(jnp.log(most) * (1.0 / LN2)) + 1.0
    scaled = jnp.round(values * jnp.exp((15.0 - power) * LN2)[None])
    scaled = jnp.minimum(jnp.maximum(scaled, -32767.0), 32767.0).reshape(XT // 2, 16, 128)
    powers = jnp.concatenate([power, jnp.zeros_like(power)], axis=0)[None]
    return jnp.concatenate([scaled, powers], axis=0).astype(jnp.int32).astype(jnp.int16)


def decode(coded):
    values = coded.astype(jnp.int32).astype(jnp.float32)
    step = jnp.exp((values[XT // 2, 0:8] - 15.0) * LN2)
    return values[:XT // 2].reshape(XT, 8, 128) * step[None]


def correlate(x_hbm, m_hbm, x_ref, nat, rows_f, rows_s, cols_s, rr, gt, hb, other, part, sent, rsr, mq, ss_l, ss_r, rs_r,
              ss_h, rs_h, ss_g, rs_g, ss_w, rs_w, ss_x, rs_x, ss_z, rs_z, ss_a, rs_a, ss_s, rs_s, ss_o):
    blk, w = lax.axis_index("blk"), lax.axis_index("walker")
    x, zh, c = blk // (NZ * NC), blk // NC % NZ, blk % NC
    y, zl = w // NL, w % NL
    z = zh * NL + zl

    def dev(x_=x, zh_=zh, c_=c, y_=y, zl_=zl):
        return ((x_ * NZ + zh_) * NC + c_, y_ * NL + zl_)

    def copy(src, dst, send, recv, to):
        return pltpu.make_async_remote_copy(
            src_ref=src, dst_ref=dst, send_sem=send, recv_sem=recv, device_id=to, device_id_type=MESH)

    def ring(at, n):
        return ([at] + [lax.rem(at + d, n) for d in range(1, n)], [at] + [lax.rem(at + n - d, n) for d in range(1, n)])

    x_peer, x_from = ring(x, NX)
    zh_peer, zh_from = ring(zh, NZ)
    y_peer, y_from = ring(y, NY)
    z_peer, z_from = ring(z, NZ * NL)
    w_peer, w_from = ring(w, NW)
    co = 1 - c
    sibling = dev(c_=co)
    sends = []

    def start(copy_):
        copy_.start()
        sends.append(copy_)

    def sent_all(since=0):
        for copy_ in sends[since:]:
            copy_.wait_send()
        del sends[since:]

    load = pltpu.make_async_copy(x_hbm, x_ref, ss_l.at[0])
    load.start()

    barrier = pltpu.get_barrier_semaphore()
    peers = [dev(zh_=z_peer[d] // NL, zl_=z_peer[d] % NL) for d in (4, 3, 5, 2, 6, 1, 7)]
    peers += [(blk, w_peer[d]) for d in range(1, NW)]
    peers += [dev(x_=x_peer[d], c_=c_) for d in (1, 2, 3) for c_ in (c, co)] + [sibling, dev(zh_=zh_peer[2], c_=co)]
    for to in peers:
        pl.semaphore_signal(barrier, inc=1, device_id=to, device_id_type=MESH)

    load.wait()
    for i in range(8):
        pair = x_ref[i // 2, i % 2].astype(jnp.float32)
        nat[i:i + 1, :] = pair[0:1]
        nat[i + 8:i + 9, :] = pair[1:2]
    for v in range(NW):
        first = 9 * (v // 2) + (5 if v % 2 else 0)
        half = 9 * (v // 2) + 4
        for i in range(4):
            rows_f[:, 32 * i:32 * i + 32] = nat[:, G * (first + i):G * (first + i) + W]
        lane = G * half + 16 * (v % 2)
        rows_f[:, 128:144] = nat[:, lane:lane + 16]
        rows_s[v] = rows_f[...].astype(jnp.bfloat16)
    zeros = jnp.zeros((16, 8), jnp.float32)
    for t in range(12):
        tile = jnp.concatenate([nat[:, 120 * t:120 * t + 120], zeros], axis=1)
        cols_s[t // 3, :, 128 * (t % 3):128 * (t % 3) + 128] = tile.astype(jnp.bfloat16)

    pl.semaphore_wait(barrier, len(peers))

    for d in range(1, NW):
        start(copy(rows_s.at[w_peer[d]], rr.at[w], ss_r.at[d], rs_r.at[d], (blk, w_peer[d])))
    for d in (1, 7, 2, 6, 3, 5, 4):
        to = z_peer[d]
        start(copy(cols_s.at[to // NL], hb.at[y, z], ss_h.at[d], rs_h.at[d], dev(zh_=to // NL, zl_=to % NL)))
    rr[w] = rows_s[w]
    hb[y, z] = cols_s[zh]

    def along_y(n):
        slot = hb.at[y, z_from[n]]
        for d in (2, 1, 3):
            start(copy(slot, slot, ss_w.at[4 * n + d], rs_w.at[4 * n + d], dev(y_=y_peer[d])))

    along_y(0)

    def arrived_h(n):
        slot = hb.at[y, z_from[n]]
        copy(slot, slot, ss_h.at[n], rs_h.at[n], dev(zh_=z_from[n] // NL, zl_=z_from[n] % NL)).wait_recv()
        along_y(n)

    for n in (1, 7, 2, 6):
        arrived_h(n)
    for d in range(1, NW):
        slot = rr.at[w_from[d]]
        copy(slot, slot, ss_r.at[d], rs_r.at[d], (blk, w_from[d])).wait_recv()
    turned = rr[...].reshape(NW * 16, 256).astype(jnp.float32).T.astype(jnp.bfloat16)
    whole = pl.multiple_of(16 * zl, 16)
    shared = pl.multiple_of(128 * (1 - zl), 16)
    gt[zh, pl.ds(whole, 128), :] = turned[0:128]
    gt[zh, pl.ds(shared, 16), :] = turned[128:144]
    for d in (2, 1, 3):
        start(copy(gt.at[zh], gt.at[zh], ss_g.at[d], rs_g.at[d], dev(zh_=zh_peer[d])))
    for n in (3, 5, 4):
        arrived_h(n)

    for n in (0, 1, 7, 2, 6, 3, 5, 4):
        for d in (1, 3, 2):
            slot = hb.at[y_from[d], z_from[n]]
            copy(slot, slot, ss_w.at[4 * n + d], rs_w.at[4 * n + d], dev(y_=y_from[d])).wait_recv()
    for d in (1, 3, 2):
        slot = gt.at[zh_from[d]]
        copy(slot, slot, ss_g.at[d], rs_g.at[d], dev(zh_=zh_from[d])).wait_recv()
    left = jnp.concatenate([gt[i] for i in range(NZ)], axis=1).astype(jnp.float32)
    lane = lax.broadcasted_iota(jnp.int32, (ROWS, NZ * 128), 1)
    real = lane % 16 < 8
    left_re = jnp.where(real, left, -left)
    left_im = jnp.where(real, pltpu.roll(left, NZ * 128 - 8, 1), pltpu.roll(left, 8, 1))
    is_re = c == 0
    mine = jnp.where(is_re, left_re, left_im).astype(jnp.bfloat16)
    theirs = jnp.where(is_re, left_im, left_re).astype(jnp.bfloat16)
    right = jnp.concatenate([hb[v // NL, i * NL + v % NL] for i in range(NZ) for v in range(NW)], axis=0)

    def tiles(left_, to):
        product = jnp.dot(left_, right, preferred_element_type=jnp.float32)
        for l in range(3):
            to[18 * l:18 * l + 18] = product[:, 128 * l:128 * l + 128].reshape(18, 8, 128)
        to[TILES:] = jnp.zeros((4 * XT - TILES, 8, 128), jnp.float32)

    def term(n, part, d, to):
        sent[n] = encode(part[pl.ds(x_peer[d] * XT, XT)])
        start(copy(sent.at[n], rsr.at[n], ss_x.at[n], rs_x.at[n], to))

    tiles(theirs, other)
    for d in (2, 1, 3, 0):
        term(4 + d, other, d, dev(x_=x_peer[d], c_=co))
    tiles(mine, part)
    for d in (2, 1, 3):
        term(d, part, d, dev(x_=x_peer[d]))
    total = part[pl.ds(x * XT, XT)]
    for n in (4, 5, 7, 1, 3, 6, 2):
        source = dev(x_=x_from[n % 4], c_=co if n >= 4 else c)
        copy(rsr.at[n], rsr.at[n], ss_x.at[n], rs_x.at[n], source).wait_recv()
        total = total + decode(rsr[n])
    mq[zh, x] = encode(total * ((2.0 * 1024) ** -0.5))

    keeps = []

    def arrived(n, d):
        at, slot = (zh_from[n], x_from[d]), mq.at[zh_from[n], x_from[d]]
        if n != 2 or d == 0:
            start(copy(slot, m_hbm.at[(c, *at)], ss_s.at[4 * n + d], rs_s.at[4 * n + d], sibling))
        keeps.append(pltpu.make_async_copy(slot, m_hbm.at[(c, *at)], ss_o.at[4 * n + d]))
        keeps[-1].start()

    def spread(n):
        slot = mq.at[zh_from[n], x]
        for d in (2, 1, 3) if n != 2 else (1, 3):
            start(copy(slot, slot, ss_a.at[4 * n + d], rs_a.at[4 * n + d], dev(x_=x_peer[d])))
            if n == 2:
                start(copy(slot, m_hbm.at[c, zh_from[n], x], ss_s.at[4 * n + d], rs_s.at[4 * n + d], dev(x_=x_peer[d], c_=co)))
        arrived(n, 0)

    def from_z(n):
        slot = mq.at[zh_from[n], x]
        copy(slot, slot, ss_z.at[n], rs_z.at[n], dev(zh_=zh_from[n])).wait_recv()
        spread(n)

    def from_x(n, d):
        slot = mq.at[zh_from[n], x_from[d]]
        source = dev(x_=x_from[d]) if (n, d) != (2, 2) else dev(zh_=zh_from[2])
        copy(slot, slot, ss_a.at[4 * n + d], rs_a.at[4 * n + d], source).wait_recv()
        arrived(n, d)

    def from_sibling(n, d):
        slot = m_hbm.at[co, zh_from[n], x_from[d]]
        copy(slot, slot, ss_s.at[4 * n + d], rs_s.at[4 * n + d], sibling).wait_recv()

    def kept():
        for copy_ in keeps:
            copy_.wait()
        del keeps[:]

    earlier = len(sends)
    slot = mq.at[zh, x]
    for d in (1, 3, 2):
        start(copy(slot, slot, ss_z.at[d], rs_z.at[d], dev(zh_=zh_peer[d])))
    spread(0)
    for copy_ in sends[:earlier]:
        copy_.wait_send()
    del sends[:earlier]
    from_z(1)
    from_z(3)
    from_x(0, 2)
    slot = mq.at[zh, x_from[2]]
    start(copy(slot, slot, ss_a.at[10], rs_a.at[10], dev(zh_=zh_peer[2])))
    start(copy(slot, m_hbm.at[c, zh, x_from[2]], ss_s.at[10], rs_s.at[10], dev(zh_=zh_peer[2], c_=co)))
    earlier = len(sends)
    from_z(2)
    from_x(0, 1)
    from_x(0, 3)
    for copy_ in sends[:earlier]:
        copy_.wait_send()
    del sends[:earlier]
    kept()
    for n, d in ((0, 0), (1, 0), (3, 0), (0, 2), (2, 0), (0, 1), (0, 3)):
        from_sibling(n, d)
    for n, d in ((1, 1), (1, 3), (1, 2), (3, 1), (3, 3), (3, 2), (2, 2), (2, 1), (2, 3)):
        from_x(n, d)
    sent_all()
    kept()
    for n, d in ((1, 1), (1, 3), (1, 2), (3, 1), (3, 3), (3, 2), (2, 2), (2, 1), (2, 3)):
        from_sibling(n, d)


def correlation(measured):
    sem = lambda n: pltpu.SemaphoreType.DMA((n,))
    return pl.pallas_call(
        correlate,
        out_shape=jax.ShapeDtypeStruct((NC, NZ, NX, HT, 16, 128), jnp.int16),
        in_specs=[pl.BlockSpec(memory_space=pltpu.HBM)],
        out_specs=pl.BlockSpec(memory_space=pltpu.HBM),
        scratch_shapes=[
            pltpu.VMEM(measured.shape, jnp.bfloat16),
            pltpu.VMEM((16, 1440), jnp.float32),
            pltpu.VMEM((16, 256), jnp.float32),
            pltpu.VMEM((NW, 16, 256), jnp.bfloat16),
            pltpu.VMEM((NZ, 16, 384), jnp.bfloat16),
            pltpu.VMEM((NW, 16, 256), jnp.bfloat16),
            pltpu.VMEM((NZ, ROWS, 128), jnp.bfloat16),
            pltpu.VMEM((NY, NZ * NL, 16, 384), jnp.bfloat16),
            pltpu.VMEM((4 * XT, 8, 128), jnp.float32),
            pltpu.VMEM((4 * XT, 8, 128), jnp.float32),
            pltpu.VMEM((NC * NX, HT, 16, 128), jnp.int16),
            pltpu.VMEM((NC * NX, HT, 16, 128), jnp.int16),
            pltpu.VMEM((NZ, NX, HT, 16, 128), jnp.int16),
            sem(1), sem(NW), sem(NW), sem(8), sem(8), sem(NZ), sem(NZ), sem(32), sem(32),
            sem(8), sem(8), sem(NZ), sem(NZ), sem(16), sem(16), sem(16), sem(16), sem(16),
        ],
        compiler_params=pltpu.CompilerParams(
            collective_id=0, has_side_effects=True, vmem_limit_bytes=60 << 20),
    )(measured)


def select(per_dev, q_hbm, nu_hbm, kq_hbm, mq_hbm, o_hbm, q_ref, nu_ref, kq_ref, mq, m_ref, o_ref, ss_l, ss_m, ss_o):
    tables = [pltpu.make_async_copy(src, dst, ss_l.at[i])
              for i, (src, dst) in enumerate(((q_hbm, q_ref), (nu_hbm, nu_ref), (kq_hbm, kq_ref)))]
    blocks = [pltpu.make_async_copy(mq_hbm.at[ri, zh], mq.at[ri, zh], ss_m.at[ri * NZ + zh])
              for ri in range(2) for zh in range(NZ)]
    for copy_ in blocks + tables:
        copy_.start()
    for ri in range(2):
        for zh in range(NZ):
            blocks[ri * NZ + zh].wait()
            for x in range(NX):
                m_ref[ri, zh, x * XT:(x + 1) * XT] = decode(mq[ri, zh, x])
    for copy_ in tables:
        copy_.wait()

    base = lax.axis_index("blk") * per_dev
    lane = lax.broadcasted_iota(jnp.int32, (18, 8, 128), 2)

    def out(tile, s):
        lanes = pl.ds(pl.multiple_of(tile * 128, 128), 128)
        return pltpu.make_async_copy(o_ref.at[tile, s], o_hbm.at[:, s, :, lanes], ss_o.at[tile * per_dev + s])

    def column_tile(tile, carry):
        for s in range(per_dev):
            q, nu = q_ref[base + s], nu_ref[base + s]
            parts = [[], []]
            for j in range(4):
                k = kq_ref[tile * 4 + j, q]
                shift = lax.rem(32 * j + 256 - (k % 3) * G - nu, 128)
                for ri in range(2):
                    block = m_ref[ri, k // 9, pl.ds(k % 9 // 3 * 18, 18)]
                    parts[ri].append(pltpu.roll(block, shift, 2))
            for ri in range(2):
                a, b, e, f = parts[ri]
                row = jnp.where(lane < 64, jnp.where(lane < 32, a, b), jnp.where(lane < 96, e, f))
                o_ref[tile, s, :, ri, :] = row.reshape(ROWS, 128)
            out(tile, s).start()
        return carry

    lax.fori_loop(0, 9, column_tile, 0, unroll=True)
    for tile in range(9):
        for s in range(per_dev):
            out(tile, s).wait()


def shards(measured, slice_q, slice_nu, kplusq):
    per_dev = slice_q.shape[0] // lax.axis_size("blk")
    sem = lambda n: pltpu.SemaphoreType.DMA((n,))
    return pl.pallas_call(
        functools.partial(select, per_dev),
        out_shape=jax.ShapeDtypeStruct((ROWS, per_dev, 2, 36 * W), jnp.float32),
        in_specs=[pl.BlockSpec(memory_space=pltpu.HBM)] * 4,
        out_specs=pl.BlockSpec(memory_space=pltpu.HBM),
        scratch_shapes=[
            pltpu.SMEM(slice_q.shape, jnp.int32),
            pltpu.SMEM(slice_nu.shape, jnp.int32),
            pltpu.SMEM(kplusq.shape, jnp.int32),
            pltpu.VMEM((NC, NZ, NX, HT, 16, 128), jnp.int16),
            pltpu.VMEM((NC, NZ, NX * XT, 8, 128), jnp.float32),
            pltpu.VMEM((9, per_dev, ROWS, 2, 128), jnp.float32),
            sem(3), sem(NC * NZ), sem(9 * per_dev),
        ],
        compiler_params=pltpu.CompilerParams(vmem_limit_bytes=60 << 20),
    )(slice_q, slice_nu, kplusq, correlation(measured))


def solution(mesh):
    return jax.shard_map(
        shards,
        mesh=mesh,
        in_specs=(P(("blk", "walker"), None, None, None), P(), P(), P()),
        out_specs=P("walker", "blk", None, None),
        check_vma=False,
    )
```

```python
import functools

import jax
import jax.numpy as jnp
from jax import lax
from jax.experimental import pallas as pl
from jax.experimental.pallas import tpu as pltpu
from jax.sharding import PartitionSpec as P

MESH = pl.DeviceIdType.MESH
W = 32
G = 40
NX, NZ, NC, NY, NL = 4, 4, 2, 4, 2
NW = NY * NL
ROWS = 144
TILES = 54
XT = 14
HT = XT // 2 + 1
LN2 = 0.6931471805599453
FAR_POWER = 64.0
FAR = 2.0 ** 64


def encode(values):
    most = jnp.maximum(jnp.max(jnp.abs(values), axis=0), 1e-37)
    power = jnp.floor(jnp.log(most) * (1.0 / LN2)) + 1.0
    scaled = jnp.round(values * FAR * jnp.exp((15.0 - FAR_POWER - power) * LN2)[None])
    scaled = jnp.minimum(jnp.maximum(scaled, -32767.0), 32767.0).reshape(XT // 2, 16, 128)
    powers = jnp.concatenate([power, jnp.zeros_like(power)], axis=0)[None]
    return jnp.concatenate([scaled, powers], axis=0).astype(jnp.int32).astype(jnp.int16)


def decode(coded):
    values = coded.astype(jnp.int32).astype(jnp.float32)
    step = jnp.exp((values[XT // 2, 0:8] - 15.0 + FAR_POWER) * LN2)
    return values[:XT // 2].reshape(XT, 8, 128) * step[None] * (1.0 / FAR)


def correlate(x_hbm, m_hbm, x_ref, nat, rows_f, rows_s, cols_s, rr, gt, hb, other, part, sent, rsr, mq, ss_l, ss_r, rs_r,
              ss_h, rs_h, ss_g, rs_g, ss_w, rs_w, ss_x, rs_x, ss_z, rs_z, ss_a, rs_a, ss_s, rs_s, ss_o):
    blk, w = lax.axis_index("blk"), lax.axis_index("walker")
    x, zh, c = blk // (NZ * NC), blk // NC % NZ, blk % NC
    y, zl = w // NL, w % NL
    z = zh * NL + zl

    def dev(x_=x, zh_=zh, c_=c, y_=y, zl_=zl):
        return ((x_ * NZ + zh_) * NC + c_, y_ * NL + zl_)

    def copy(src, dst, send, recv, to):
        return pltpu.make_async_remote_copy(
            src_ref=src, dst_ref=dst, send_sem=send, recv_sem=recv, device_id=to, device_id_type=MESH)

    def ring(at, n):
        return ([at] + [lax.rem(at + d, n) for d in range(1, n)], [at] + [lax.rem(at + n - d, n) for d in range(1, n)])

    x_peer, x_from = ring(x, NX)
    zh_peer, zh_from = ring(zh, NZ)
    y_peer, y_from = ring(y, NY)
    z_peer, z_from = ring(z, NZ * NL)
    w_peer, w_from = ring(w, NW)
    co = 1 - c
    sibling = dev(c_=co)
    sends = []

    def start(copy_):
        copy_.start()
        sends.append(copy_)

    def sent_all(since=0):
        for copy_ in sends[since:]:
            copy_.wait_send()
        del sends[since:]

    load = pltpu.make_async_copy(x_hbm, x_ref, ss_l.at[0])
    load.start()

    barrier = pltpu.get_barrier_semaphore()
    peers = [dev(zh_=z_peer[d] // NL, zl_=z_peer[d] % NL) for d in (4, 3, 5, 2, 6, 1, 7)]
    peers += [(blk, w_peer[d]) for d in range(1, NW)]
    peers += [dev(x_=x_peer[d], c_=c_) for d in (1, 2, 3) for c_ in (c, co)] + [sibling, dev(zh_=zh_peer[2], c_=co)]
    for to in peers:
        pl.semaphore_signal(barrier, inc=1, device_id=to, device_id_type=MESH)

    load.wait()
    for i in range(8):
        pair = x_ref[i // 2, i % 2].astype(jnp.float32)
        nat[i:i + 1, :] = pair[0:1]
        nat[i + 8:i + 9, :] = pair[1:2]
    for v in range(NW):
        first = 9 * (v // 2) + (5 if v % 2 else 0)
        half = 9 * (v // 2) + 4
        for i in range(4):
            rows_f[:, 32 * i:32 * i + 32] = nat[:, G * (first + i):G * (first + i) + W]
        lane = G * half + 16 * (v % 2)
        rows_f[:, 128:144] = nat[:, lane:lane + 16]
        rows_s[v] = rows_f[...].astype(jnp.bfloat16)
    zeros = jnp.zeros((16, 8), jnp.float32)
    for t in range(12):
        tile = jnp.concatenate([nat[:, 120 * t:120 * t + 120], zeros], axis=1)
        cols_s[t // 3, :, 128 * (t % 3):128 * (t % 3) + 128] = tile.astype(jnp.bfloat16)

    pl.semaphore_wait(barrier, len(peers))

    for d in range(1, NW):
        start(copy(rows_s.at[w_peer[d]], rr.at[w], ss_r.at[d], rs_r.at[d], (blk, w_peer[d])))
    for d in (1, 7, 2, 6, 3, 5, 4):
        to = z_peer[d]
        start(copy(cols_s.at[to // NL], hb.at[y, z], ss_h.at[d], rs_h.at[d], dev(zh_=to // NL, zl_=to % NL)))
    rr[w] = rows_s[w]
    hb[y, z] = cols_s[zh]

    def along_y(n):
        slot = hb.at[y, z_from[n]]
        for d in (2, 1, 3):
            start(copy(slot, slot, ss_w.at[4 * n + d], rs_w.at[4 * n + d], dev(y_=y_peer[d])))

    along_y(0)

    def arrived_h(n):
        slot = hb.at[y, z_from[n]]
        copy(slot, slot, ss_h.at[n], rs_h.at[n], dev(zh_=z_from[n] // NL, zl_=z_from[n] % NL)).wait_recv()
        along_y(n)

    for n in (1, 7, 2, 6):
        arrived_h(n)
    for d in range(1, NW):
        slot = rr.at[w_from[d]]
        copy(slot, slot, ss_r.at[d], rs_r.at[d], (blk, w_from[d])).wait_recv()
    turned = rr[...].reshape(NW * 16, 256).astype(jnp.float32).T.astype(jnp.bfloat16)
    whole = pl.multiple_of(16 * zl, 16)
    shared = pl.multiple_of(128 * (1 - zl), 16)
    gt[zh, pl.ds(whole, 128), :] = turned[0:128]
    gt[zh, pl.ds(shared, 16), :] = turned[128:144]
    for d in (2, 1, 3):
        start(copy(gt.at[zh], gt.at[zh], ss_g.at[d], rs_g.at[d], dev(zh_=zh_peer[d])))
    for n in (3, 5, 4):
        arrived_h(n)

    def term(n, part_, d, to):
        sent[n] = encode(part_[pl.ds(x_peer[d] * XT, XT)])
        start(copy(sent.at[n], rsr.at[n], ss_x.at[n], rs_x.at[n], to))

    def add(left_, right_, to, first):
        product = jnp.dot(left_.astype(jnp.bfloat16), right_, preferred_element_type=jnp.float32)
        for l in range(3):
            tiles = product[:, 128 * l:128 * l + 128].reshape(18, 8, 128)
            to[18 * l:18 * l + 18] = tiles if first else to[18 * l:18 * l + 18] + tiles

    other[TILES:] = jnp.zeros((4 * XT - TILES, 8, 128), jnp.float32)
    part[TILES:] = jnp.zeros((4 * XT - TILES, 8, 128), jnp.float32)
    real = lax.broadcasted_iota(jnp.int32, (ROWS, 128), 1) % 16 < 8
    is_re = c == 0
    for n in (0, 1, 3, 2):
        at = zh_from[n]
        for l in range(NL):
            apart = lax.rem(z - (at * NL + l) + 8, 8)
            for d in (1, 3, 2):
                slot = hb.at[y_from[d], at * NL + l]
                copy(slot, slot, ss_w.at[4 * apart + d], rs_w.at[4 * apart + d], dev(y_=y_from[d])).wait_recv()
        if n:
            copy(gt.at[at], gt.at[at], ss_g.at[n], rs_g.at[n], dev(zh_=at)).wait_recv()
        left = gt[at].astype(jnp.float32)
        left_re = jnp.where(real, left, -left)
        left_im = jnp.where(real, pltpu.roll(left, 120, 1), pltpu.roll(left, 8, 1))
        right = jnp.concatenate([hb[v // NL, at * NL + v % NL] for v in range(NW)], axis=0)
        add(jnp.where(is_re, left_im, left_re), right, other, n == 0)
        if n == 2:
            for d in (2, 1, 3, 0):
                term(4 + d, other, d, dev(x_=x_peer[d], c_=co))
        add(jnp.where(is_re, left_re, left_im), right, part, n == 0)
    for d in (2, 1, 3):
        term(d, part, d, dev(x_=x_peer[d]))
    total = part[pl.ds(x * XT, XT)]
    for n in (4, 5, 7, 1, 3, 6, 2):
        source = dev(x_=x_from[n % 4], c_=co if n >= 4 else c)
        copy(rsr.at[n], rsr.at[n], ss_x.at[n], rs_x.at[n], source).wait_recv()
        total = total + decode(rsr[n])
    mq[zh, x] = encode(total * ((2.0 * 1024) ** -0.5))

    keeps = []

    def arrived(n, d):
        at, slot = (zh_from[n], x_from[d]), mq.at[zh_from[n], x_from[d]]
        if n != 2 or d == 0:
            start(copy(slot, m_hbm.at[(c, *at)], ss_s.at[4 * n + d], rs_s.at[4 * n + d], sibling))
        keeps.append(pltpu.make_async_copy(slot, m_hbm.at[(c, *at)], ss_o.at[4 * n + d]))
        keeps[-1].start()

    def spread(n):
        slot = mq.at[zh_from[n], x]
        for d in (2, 1, 3) if n != 2 else (1, 3):
            start(copy(slot, slot, ss_a.at[4 * n + d], rs_a.at[4 * n + d], dev(x_=x_peer[d])))
            if n == 2:
                start(copy(slot, m_hbm.at[c, zh_from[n], x], ss_s.at[4 * n + d], rs_s.at[4 * n + d], dev(x_=x_peer[d], c_=co)))
        arrived(n, 0)

    def from_z(n):
        slot = mq.at[zh_from[n], x]
        copy(slot, slot, ss_z.at[n], rs_z.at[n], dev(zh_=zh_from[n])).wait_recv()
        spread(n)

    def from_x(n, d):
        slot = mq.at[zh_from[n], x_from[d]]
        source = dev(x_=x_from[d]) if (n, d) != (2, 2) else dev(zh_=zh_from[2])
        copy(slot, slot, ss_a.at[4 * n + d], rs_a.at[4 * n + d], source).wait_recv()
        arrived(n, d)

    def from_sibling(n, d):
        slot = m_hbm.at[co, zh_from[n], x_from[d]]
        copy(slot, slot, ss_s.at[4 * n + d], rs_s.at[4 * n + d], sibling).wait_recv()

    def kept():
        for copy_ in keeps:
            copy_.wait()
        del keeps[:]

    earlier = len(sends)
    slot = mq.at[zh, x]
    for d in (1, 3, 2):
        start(copy(slot, slot, ss_z.at[d], rs_z.at[d], dev(zh_=zh_peer[d])))
    spread(0)
    for copy_ in sends[:earlier]:
        copy_.wait_send()
    del sends[:earlier]
    from_z(1)
    from_z(3)
    from_x(0, 2)
    slot = mq.at[zh, x_from[2]]
    start(copy(slot, slot, ss_a.at[10], rs_a.at[10], dev(zh_=zh_peer[2])))
    start(copy(slot, m_hbm.at[c, zh, x_from[2]], ss_s.at[10], rs_s.at[10], dev(zh_=zh_peer[2], c_=co)))
    earlier = len(sends)
    from_z(2)
    from_x(0, 1)
    from_x(0, 3)
    for copy_ in sends[:earlier]:
        copy_.wait_send()
    del sends[:earlier]
    kept()
    for n, d in ((0, 0), (1, 0), (3, 0), (0, 2), (2, 0), (0, 1), (0, 3)):
        from_sibling(n, d)
    for n, d in ((1, 1), (1, 3), (1, 2), (3, 1), (3, 3), (3, 2), (2, 2), (2, 1), (2, 3)):
        from_x(n, d)
    sent_all()
    kept()
    for n, d in ((1, 1), (1, 3), (1, 2), (3, 1), (3, 3), (3, 2), (2, 2), (2, 1), (2, 3)):
        from_sibling(n, d)


def correlation(measured):
    sem = lambda n: pltpu.SemaphoreType.DMA((n,))
    return pl.pallas_call(
        correlate,
        out_shape=jax.ShapeDtypeStruct((NC, NZ, NX, HT, 16, 128), jnp.int16),
        in_specs=[pl.BlockSpec(memory_space=pltpu.HBM)],
        out_specs=pl.BlockSpec(memory_space=pltpu.HBM),
        scratch_shapes=[
            pltpu.VMEM(measured.shape, jnp.bfloat16),
            pltpu.VMEM((16, 1440), jnp.float32),
            pltpu.VMEM((16, 256), jnp.float32),
            pltpu.VMEM((NW, 16, 256), jnp.bfloat16),
            pltpu.VMEM((NZ, 16, 384), jnp.bfloat16),
            pltpu.VMEM((NW, 16, 256), jnp.bfloat16),
            pltpu.VMEM((NZ, ROWS, 128), jnp.bfloat16),
            pltpu.VMEM((NY, NZ * NL, 16, 384), jnp.bfloat16),
            pltpu.VMEM((4 * XT, 8, 128), jnp.float32),
            pltpu.VMEM((4 * XT, 8, 128), jnp.float32),
            pltpu.VMEM((NC * NX, HT, 16, 128), jnp.int16),
            pltpu.VMEM((NC * NX, HT, 16, 128), jnp.int16),
            pltpu.VMEM((NZ, NX, HT, 16, 128), jnp.int16),
            sem(1), sem(NW), sem(NW), sem(8), sem(8), sem(NZ), sem(NZ), sem(32), sem(32),
            sem(8), sem(8), sem(NZ), sem(NZ), sem(16), sem(16), sem(16), sem(16), sem(16),
        ],
        compiler_params=pltpu.CompilerParams(
            collective_id=0, has_side_effects=True, vmem_limit_bytes=60 << 20),
    )(measured)


def select(per_dev, q_hbm, nu_hbm, kq_hbm, mq_hbm, o_hbm, q_ref, nu_ref, kq_ref, mq, m_ref, o_ref, ss_l, ss_m, ss_o):
    tables = [pltpu.make_async_copy(src, dst, ss_l.at[i])
              for i, (src, dst) in enumerate(((q_hbm, q_ref), (nu_hbm, nu_ref), (kq_hbm, kq_ref)))]
    blocks = [pltpu.make_async_copy(mq_hbm.at[ri, zh], mq.at[ri, zh], ss_m.at[ri * NZ + zh])
              for ri in range(2) for zh in range(NZ)]
    for copy_ in blocks + tables:
        copy_.start()
    for ri in range(2):
        for zh in range(NZ):
            blocks[ri * NZ + zh].wait()
            for x in range(NX):
                m_ref[ri, zh, x * XT:(x + 1) * XT] = decode(mq[ri, zh, x])
    for copy_ in tables:
        copy_.wait()

    base = lax.axis_index("blk") * per_dev
    lane = lax.broadcasted_iota(jnp.int32, (18, 8, 128), 2)

    def out(tile, s):
        lanes = pl.ds(pl.multiple_of(tile * 128, 128), 128)
        return pltpu.make_async_copy(o_ref.at[tile, s], o_hbm.at[:, s, :, lanes], ss_o.at[tile * per_dev + s])

    def column_tile(tile, carry):
        for s in range(per_dev):
            q, nu = q_ref[base + s], nu_ref[base + s]
            parts = [[], []]
            for j in range(4):
                k = kq_ref[tile * 4 + j, q]
                shift = lax.rem(32 * j + 256 - (k % 3) * G - nu, 128)
                for ri in range(2):
                    block = m_ref[ri, k // 9, pl.ds(k % 9 // 3 * 18, 18)]
                    parts[ri].append(pltpu.roll(block, shift, 2))
            for ri in range(2):
                a, b, e, f = parts[ri]
                row = jnp.where(lane < 64, jnp.where(lane < 32, a, b), jnp.where(lane < 96, e, f))
                o_ref[tile, s, :, ri, :] = row.reshape(ROWS, 128)
            out(tile, s).start()
        return carry

    lax.fori_loop(0, 9, column_tile, 0, unroll=True)
    for tile in range(9):
        for s in range(per_dev):
            out(tile, s).wait()


def shards(measured, slice_q, slice_nu, kplusq):
    per_dev = slice_q.shape[0] // lax.axis_size("blk")
    sem = lambda n: pltpu.SemaphoreType.DMA((n,))
    return pl.pallas_call(
        functools.partial(select, per_dev),
        out_shape=jax.ShapeDtypeStruct((ROWS, per_dev, 2, 36 * W), jnp.float32),
        in_specs=[pl.BlockSpec(memory_space=pltpu.HBM)] * 4,
        out_specs=pl.BlockSpec(memory_space=pltpu.HBM),
        scratch_shapes=[
            pltpu.SMEM(slice_q.shape, jnp.int32),
            pltpu.SMEM(slice_nu.shape, jnp.int32),
            pltpu.SMEM(kplusq.shape, jnp.int32),
            pltpu.VMEM((NC, NZ, NX, HT, 16, 128), jnp.int16),
            pltpu.VMEM((NC, NZ, NX * XT, 8, 128), jnp.float32),
            pltpu.VMEM((9, per_dev, ROWS, 2, 128), jnp.float32),
            sem(3), sem(NC * NZ), sem(9 * per_dev),
        ],
        compiler_params=pltpu.CompilerParams(vmem_limit_bytes=60 << 20),
    )(slice_q, slice_nu, kplusq, correlation(measured))


def solution(mesh):
    return jax.shard_map(
        shards,
        mesh=mesh,
        in_specs=(P(("blk", "walker"), None, None, None), P(), P(), P()),
        out_specs=P("walker", "blk", None, None),
        check_vma=False,
    )
```

```python
import functools

import jax
import jax.numpy as jnp
from jax import lax
from jax.experimental import pallas as pl
from jax.experimental.pallas import tpu as pltpu
from jax.sharding import PartitionSpec as P

MESH = pl.DeviceIdType.MESH
W = 32
G = 40
NX, NZ, NC, NY, NL = 4, 4, 2, 4, 2
NW = NY * NL
ROWS = 144
TILES = 54
XT = 14
HT = XT // 2 + 1
LN2 = 0.6931471805599453
FAR_POWER = 64.0
FAR = 2.0 ** 64


def encode(values):
    most = jnp.maximum(jnp.max(jnp.abs(values), axis=0), 1e-37)
    power = jnp.floor(jnp.log(most) * (1.0 / LN2)) + 1.0
    scaled = jnp.round(values * FAR * jnp.exp((15.0 - FAR_POWER - power) * LN2)[None])
    scaled = jnp.minimum(jnp.maximum(scaled, -32767.0), 32767.0).reshape(XT // 2, 16, 128)
    powers = jnp.concatenate([power, jnp.zeros_like(power)], axis=0)[None]
    return jnp.concatenate([scaled, powers], axis=0).astype(jnp.int32).astype(jnp.int16)


def decode(coded):
    values = coded.astype(jnp.int32).astype(jnp.float32)
    step = jnp.exp((values[XT // 2, 0:8] - 15.0 + FAR_POWER) * LN2)
    return values[:XT // 2].reshape(XT, 8, 128) * step[None] * (1.0 / FAR)


def correlate(x_hbm, m_hbm, x_ref, nat, rows_f, rows_s, cols_s, rr, gt, hb, other, part, sent, rsr, mq, ss_l, ss_r, rs_r,
              ss_h, rs_h, ss_g, rs_g, ss_w, rs_w, ss_x, rs_x, ss_z, rs_z, ss_a, rs_a, ss_s, rs_s, ss_o):
    blk, w = lax.axis_index("blk"), lax.axis_index("walker")
    x, zh, c = blk // (NZ * NC), blk // NC % NZ, blk % NC
    y, zl = w // NL, w % NL
    z = zh * NL + zl

    def dev(x_=x, zh_=zh, c_=c, y_=y, zl_=zl):
        return ((x_ * NZ + zh_) * NC + c_, y_ * NL + zl_)

    def copy(src, dst, send, recv, to):
        return pltpu.make_async_remote_copy(
            src_ref=src, dst_ref=dst, send_sem=send, recv_sem=recv, device_id=to, device_id_type=MESH)

    def ring(at, n):
        return ([at] + [lax.rem(at + d, n) for d in range(1, n)], [at] + [lax.rem(at + n - d, n) for d in range(1, n)])

    x_peer, x_from = ring(x, NX)
    zh_peer, zh_from = ring(zh, NZ)
    y_peer, y_from = ring(y, NY)
    z_peer, z_from = ring(z, NZ * NL)
    w_peer, w_from = ring(w, NW)
    co = 1 - c
    sibling = dev(c_=co)
    sends = []

    def start(copy_):
        copy_.start()
        sends.append(copy_)

    def sent_all(since=0):
        for copy_ in sends[since:]:
            copy_.wait_send()
        del sends[since:]

    load = pltpu.make_async_copy(x_hbm, x_ref, ss_l.at[0])
    load.start()

    barrier = pltpu.get_barrier_semaphore()
    peers = [dev(zh_=z_peer[d] // NL, zl_=z_peer[d] % NL) for d in (4, 3, 5, 2, 6, 1, 7)]
    peers += [(blk, w_peer[d]) for d in range(1, NW)]
    peers += [dev(x_=x_peer[d], c_=c_) for d in (1, 2, 3) for c_ in (c, co)] + [sibling, dev(zh_=zh_peer[2], c_=co)]
    for to in peers:
        pl.semaphore_signal(barrier, inc=1, device_id=to, device_id_type=MESH)

    load.wait()
    for i in range(8):
        pair = x_ref[i // 2, i % 2].astype(jnp.float32)
        nat[i:i + 1, :] = pair[0:1]
        nat[i + 8:i + 9, :] = pair[1:2]
    for v in range(NW):
        first = 9 * (v // 2) + (5 if v % 2 else 0)
        half = 9 * (v // 2) + 4
        for i in range(4):
            rows_f[:, 32 * i:32 * i + 32] = nat[:, G * (first + i):G * (first + i) + W]
        lane = G * half + 16 * (v % 2)
        rows_f[:, 128:144] = nat[:, lane:lane + 16]
        rows_s[v] = rows_f[...].astype(jnp.bfloat16)
    zeros = jnp.zeros((16, 8), jnp.float32)
    for t in range(12):
        tile = jnp.concatenate([nat[:, 120 * t:120 * t + 120], zeros], axis=1)
        cols_s[t // 3, :, 128 * (t % 3):128 * (t % 3) + 128] = tile.astype(jnp.bfloat16)

    pl.semaphore_wait(barrier, len(peers))

    for d in range(1, NW):
        start(copy(rows_s.at[w_peer[d]], rr.at[w], ss_r.at[d], rs_r.at[d], (blk, w_peer[d])))
    for d in (1, 7, 2, 6, 3, 5, 4):
        to = z_peer[d]
        start(copy(cols_s.at[to // NL], hb.at[y, z], ss_h.at[d], rs_h.at[d], dev(zh_=to // NL, zl_=to % NL)))
    rr[w] = rows_s[w]
    hb[y, z] = cols_s[zh]

    def along_y(n):
        slot = hb.at[y, z_from[n]]
        for d in (2, 1, 3):
            start(copy(slot, slot, ss_w.at[4 * n + d], rs_w.at[4 * n + d], dev(y_=y_peer[d])))

    along_y(0)

    def arrived_h(n):
        slot = hb.at[y, z_from[n]]
        copy(slot, slot, ss_h.at[n], rs_h.at[n], dev(zh_=z_from[n] // NL, zl_=z_from[n] % NL)).wait_recv()
        along_y(n)

    for n in (1, 7, 2, 6):
        arrived_h(n)
    for d in range(1, NW):
        slot = rr.at[w_from[d]]
        copy(slot, slot, ss_r.at[d], rs_r.at[d], (blk, w_from[d])).wait_recv()
    turned = rr[...].reshape(NW * 16, 256).astype(jnp.float32).T.astype(jnp.bfloat16)
    whole = pl.multiple_of(16 * zl, 16)
    shared = pl.multiple_of(128 * (1 - zl), 16)
    gt[zh, pl.ds(whole, 128), :] = turned[0:128]
    gt[zh, pl.ds(shared, 16), :] = turned[128:144]
    for d in (2, 1, 3):
        start(copy(gt.at[zh], gt.at[zh], ss_g.at[d], rs_g.at[d], dev(zh_=zh_peer[d])))
    for n in (3, 5, 4):
        arrived_h(n)

    def term(n, part_, d, to):
        sent[n] = encode(part_[pl.ds(x_peer[d] * XT, XT)])
        start(copy(sent.at[n], rsr.at[n], ss_x.at[n], rs_x.at[n], to))

    def add(left_, right_, to, first):
        product = jnp.dot(left_.astype(jnp.bfloat16), right_, preferred_element_type=jnp.float32)
        for l in range(3):
            tiles = product[:, 128 * l:128 * l + 128].reshape(18, 8, 128)
            to[18 * l:18 * l + 18] = tiles if first else to[18 * l:18 * l + 18] + tiles

    other[TILES:] = jnp.zeros((4 * XT - TILES, 8, 128), jnp.float32)
    part[TILES:] = jnp.zeros((4 * XT - TILES, 8, 128), jnp.float32)
    real = lax.broadcasted_iota(jnp.int32, (ROWS, 128), 1) % 16 < 8
    is_re = c == 0
    for n in (0, 1, 3, 2):
        at = zh_from[n]
        for l in range(NL):
            apart = lax.rem(z - (at * NL + l) + 8, 8)
            for d in (1, 3, 2):
                slot = hb.at[y_from[d], at * NL + l]
                copy(slot, slot, ss_w.at[4 * apart + d], rs_w.at[4 * apart + d], dev(y_=y_from[d])).wait_recv()
        if n:
            copy(gt.at[at], gt.at[at], ss_g.at[n], rs_g.at[n], dev(zh_=at)).wait_recv()
        left = gt[at].astype(jnp.float32)
        left_re = jnp.where(real, left, -left)
        left_im = jnp.where(real, pltpu.roll(left, 120, 1), pltpu.roll(left, 8, 1))
        right = jnp.concatenate([hb[v // NL, at * NL + v % NL] for v in range(NW)], axis=0)
        add(jnp.where(is_re, left_im, left_re), right, other, n == 0)
        add(jnp.where(is_re, left_re, left_im), right, part, n == 0)
    for d in (2, 1, 3):
        term(4 + d, other, d, dev(x_=x_peer[d], c_=co))
        term(d, part, d, dev(x_=x_peer[d]))
    term(4, other, 0, sibling)
    total = part[pl.ds(x * XT, XT)]
    for n in (4, 5, 7, 1, 3, 6, 2):
        source = dev(x_=x_from[n % 4], c_=co if n >= 4 else c)
        copy(rsr.at[n], rsr.at[n], ss_x.at[n], rs_x.at[n], source).wait_recv()
        total = total + decode(rsr[n])
    mq[zh, x] = encode(total * ((2.0 * 1024) ** -0.5))

    keeps = []

    def arrived(n, d):
        at, slot = (zh_from[n], x_from[d]), mq.at[zh_from[n], x_from[d]]
        if n != 2 or d == 0:
            start(copy(slot, m_hbm.at[(c, *at)], ss_s.at[4 * n + d], rs_s.at[4 * n + d], sibling))
        keeps.append(pltpu.make_async_copy(slot, m_hbm.at[(c, *at)], ss_o.at[4 * n + d]))
        keeps[-1].start()

    def spread(n):
        slot = mq.at[zh_from[n], x]
        for d in (2, 1, 3) if n != 2 else (1, 3):
            start(copy(slot, slot, ss_a.at[4 * n + d], rs_a.at[4 * n + d], dev(x_=x_peer[d])))
            if n == 2:
                start(copy(slot, m_hbm.at[c, zh_from[n], x], ss_s.at[4 * n + d], rs_s.at[4 * n + d], dev(x_=x_peer[d], c_=co)))
        arrived(n, 0)

    def from_z(n):
        slot = mq.at[zh_from[n], x]
        copy(slot, slot, ss_z.at[n], rs_z.at[n], dev(zh_=zh_from[n])).wait_recv()
        spread(n)

    def from_x(n, d):
        slot = mq.at[zh_from[n], x_from[d]]
        source = dev(x_=x_from[d]) if (n, d) != (2, 2) else dev(zh_=zh_from[2])
        copy(slot, slot, ss_a.at[4 * n + d], rs_a.at[4 * n + d], source).wait_recv()
        arrived(n, d)

    def from_sibling(n, d):
        slot = m_hbm.at[co, zh_from[n], x_from[d]]
        copy(slot, slot, ss_s.at[4 * n + d], rs_s.at[4 * n + d], sibling).wait_recv()

    def kept():
        for copy_ in keeps:
            copy_.wait()
        del keeps[:]

    earlier = len(sends)
    slot = mq.at[zh, x]
    for d in (1, 3, 2):
        start(copy(slot, slot, ss_z.at[d], rs_z.at[d], dev(zh_=zh_peer[d])))
    spread(0)
    for copy_ in sends[:earlier]:
        copy_.wait_send()
    del sends[:earlier]
    from_z(1)
    from_z(3)
    from_x(0, 2)
    slot = mq.at[zh, x_from[2]]
    start(copy(slot, slot, ss_a.at[10], rs_a.at[10], dev(zh_=zh_peer[2])))
    start(copy(slot, m_hbm.at[c, zh, x_from[2]], ss_s.at[10], rs_s.at[10], dev(zh_=zh_peer[2], c_=co)))
    earlier = len(sends)
    from_z(2)
    from_x(0, 1)
    from_x(0, 3)
    for copy_ in sends[:earlier]:
        copy_.wait_send()
    del sends[:earlier]
    kept()
    for n, d in ((0, 0), (1, 0), (3, 0), (0, 2), (2, 0), (0, 1), (0, 3)):
        from_sibling(n, d)
    for n, d in ((1, 1), (1, 3), (1, 2), (3, 1), (3, 3), (3, 2), (2, 2), (2, 1), (2, 3)):
        from_x(n, d)
    sent_all()
    kept()
    for n, d in ((1, 1), (1, 3), (1, 2), (3, 1), (3, 3), (3, 2), (2, 2), (2, 1), (2, 3)):
        from_sibling(n, d)


def correlation(measured):
    sem = lambda n: pltpu.SemaphoreType.DMA((n,))
    return pl.pallas_call(
        correlate,
        out_shape=jax.ShapeDtypeStruct((NC, NZ, NX, HT, 16, 128), jnp.int16),
        in_specs=[pl.BlockSpec(memory_space=pltpu.HBM)],
        out_specs=pl.BlockSpec(memory_space=pltpu.HBM),
        scratch_shapes=[
            pltpu.VMEM(measured.shape, jnp.bfloat16),
            pltpu.VMEM((16, 1440), jnp.float32),
            pltpu.VMEM((16, 256), jnp.float32),
            pltpu.VMEM((NW, 16, 256), jnp.bfloat16),
            pltpu.VMEM((NZ, 16, 384), jnp.bfloat16),
            pltpu.VMEM((NW, 16, 256), jnp.bfloat16),
            pltpu.VMEM((NZ, ROWS, 128), jnp.bfloat16),
            pltpu.VMEM((NY, NZ * NL, 16, 384), jnp.bfloat16),
            pltpu.VMEM((4 * XT, 8, 128), jnp.float32),
            pltpu.VMEM((4 * XT, 8, 128), jnp.float32),
            pltpu.VMEM((NC * NX, HT, 16, 128), jnp.int16),
            pltpu.VMEM((NC * NX, HT, 16, 128), jnp.int16),
            pltpu.VMEM((NZ, NX, HT, 16, 128), jnp.int16),
            sem(1), sem(NW), sem(NW), sem(8), sem(8), sem(NZ), sem(NZ), sem(32), sem(32),
            sem(8), sem(8), sem(NZ), sem(NZ), sem(16), sem(16), sem(16), sem(16), sem(16),
        ],
        compiler_params=pltpu.CompilerParams(
            collective_id=0, has_side_effects=True, vmem_limit_bytes=60 << 20),
    )(measured)


def select(per_dev, q_hbm, nu_hbm, kq_hbm, mq_hbm, o_hbm, q_ref, nu_ref, kq_ref, mq, m_ref, o_ref, ss_l, ss_m, ss_o):
    tables = [pltpu.make_async_copy(src, dst, ss_l.at[i])
              for i, (src, dst) in enumerate(((q_hbm, q_ref), (nu_hbm, nu_ref), (kq_hbm, kq_ref)))]
    blocks = [pltpu.make_async_copy(mq_hbm.at[ri, zh], mq.at[ri, zh], ss_m.at[ri * NZ + zh])
              for ri in range(2) for zh in range(NZ)]
    for copy_ in blocks + tables:
        copy_.start()
    for ri in range(2):
        for zh in range(NZ):
            blocks[ri * NZ + zh].wait()
            for x in range(NX):
                m_ref[ri, zh, x * XT:(x + 1) * XT] = decode(mq[ri, zh, x])
    for copy_ in tables:
        copy_.wait()

    base = lax.axis_index("blk") * per_dev
    lane = lax.broadcasted_iota(jnp.int32, (18, 8, 128), 2)

    def out(tile, s):
        lanes = pl.ds(pl.multiple_of(tile * 128, 128), 128)
        return pltpu.make_async_copy(o_ref.at[tile, s], o_hbm.at[:, s, :, lanes], ss_o.at[tile * per_dev + s])

    def column_tile(tile, carry):
        for s in range(per_dev):
            q, nu = q_ref[base + s], nu_ref[base + s]
            parts = [[], []]
            for j in range(4):
                k = kq_ref[tile * 4 + j, q]
                shift = lax.rem(32 * j + 256 - (k % 3) * G - nu, 128)
                for ri in range(2):
                    block = m_ref[ri, k // 9, pl.ds(k % 9 // 3 * 18, 18)]
                    parts[ri].append(pltpu.roll(block, shift, 2))
            for ri in range(2):
                a, b, e, f = parts[ri]
                row = jnp.where(lane < 64, jnp.where(lane < 32, a, b), jnp.where(lane < 96, e, f))
                o_ref[tile, s, :, ri, :] = row.reshape(ROWS, 128)
            out(tile, s).start()
        return carry

    lax.fori_loop(0, 9, column_tile, 0, unroll=True)
    for tile in range(9):
        for s in range(per_dev):
            out(tile, s).wait()


def shards(measured, slice_q, slice_nu, kplusq):
    per_dev = slice_q.shape[0] // lax.axis_size("blk")
    sem = lambda n: pltpu.SemaphoreType.DMA((n,))
    return pl.pallas_call(
        functools.partial(select, per_dev),
        out_shape=jax.ShapeDtypeStruct((ROWS, per_dev, 2, 36 * W), jnp.float32),
        in_specs=[pl.BlockSpec(memory_space=pltpu.HBM)] * 4,
        out_specs=pl.BlockSpec(memory_space=pltpu.HBM),
        scratch_shapes=[
            pltpu.SMEM(slice_q.shape, jnp.int32),
            pltpu.SMEM(slice_nu.shape, jnp.int32),
            pltpu.SMEM(kplusq.shape, jnp.int32),
            pltpu.VMEM((NC, NZ, NX, HT, 16, 128), jnp.int16),
            pltpu.VMEM((NC, NZ, NX * XT, 8, 128), jnp.float32),
            pltpu.VMEM((9, per_dev, ROWS, 2, 128), jnp.float32),
            sem(3), sem(NC * NZ), sem(9 * per_dev),
        ],
        compiler_params=pltpu.CompilerParams(vmem_limit_bytes=60 << 20),
    )(slice_q, slice_nu, kplusq, correlation(measured))


def solution(mesh):
    return jax.shard_map(
        shards,
        mesh=mesh,
        in_specs=(P(("blk", "walker"), None, None, None), P(), P(), P()),
        out_specs=P("walker", "blk", None, None),
        check_vma=False,
    )
```
